32 devices in a mesh: slab: 2 (over x), cell: 8 (over z, y), dp: 2 (over core).
Axes of the slice: x: 2, y: 2, z: 4, core: 2. Of those that a mesh axis runs over, the one named last changes fastest.
Arguments:
- sens: float32 [2, 2048, 32768], P(None, ('slab', 'dp'), 'cell'), parts along dimension 1, may hold values from -0.03125 to 0.03125
- observed: float32 [2, 2048], P(None, ('slab', 'dp')), parts along dimension 1, may hold values from -6 to 6
- noise: float32 [2, 2048], P(None, ('slab', 'dp')), parts along dimension 1, may hold values from 0.5 to 2
- survey_ids: int32 [2, 2048], P(None, ('slab', 'dp')), parts along dimension 1, may hold values from 0 to 7
- data_perturb: float32 [2, 8, 2048], P(None, None, ('slab', 'dp')), parts along dimension 2, may hold values from -6 to 6
- prior: float32 [2, 16, 32, 1024], P(None, 'slab', 'cell'), parts along dimension 1, may hold values from -6 to 6
Outputs:
- models: float32 [2, 16, 32, 1024], P(None, 'slab', 'cell'), parts along dimension 1
The draws below stay inside these ranges and needn't reach their ends.
There are 2 independent parts, one for each index of `slab`. The reference program is written for one: setup_inputs(seed, part) draws one part's arguments, and reference() takes and returns one part's arrays. A program takes and returns all parts, laid end to end along the dimension named above; each array names one. Nothing has to cross between parts.
All inputs are finite; a program needn't handle non-finite values.
Results may differ from the reference program's by a relative error of at most 0.0001.
Values sent between devices are 32-bit elements; how exact they have to be, the bound alone decides.
No kernel may reach another device: no remote copies, remote signals or barrier semaphores. Data moves between devices by JAX's collectives and lax.ppermute only.
A program may use at most 64 MiB of HBM per device.

```python
import math
import jax
import jax.numpy as jnp
from jax import lax

NX = 32
NY = 32
NZ = 32
MODELS = 8
NSURV = 8
ITERS = 4
ND = 1024
NC = 32768


def set_ends(values, key, smallest, high):
    shape = values.shape
    spot = [jax.random.randint(jax.random.fold_in(key, axis), (), 0, shape[axis]) for axis in range(len(shape))]
    values = values.at[tuple(spot)].set(smallest)
    longest = shape.index(max(shape))
    spot[longest] = (spot[longest] + 1) % shape[longest]
    return values.at[tuple(spot)].set(high)


def shard_levels(rng, shape, shards, least, largest):
    def one(dim, blocks):
        steps = jax.random.uniform(jax.random.fold_in(jax.random.fold_in(rng, 6), dim), (blocks,), jnp.float32, least / len(shards), largest / len(shards))
        return jnp.repeat(jnp.exp(steps), shape[dim] // blocks).reshape((-1,) + (1,) * (len(shape) - dim - 1))

    loudness = one(*shards[0])
    for cut in shards[1:]:
        loudness = loudness * one(*cut)
    return loudness


def normal_values(stream_key, shape, scale, most, split=(), kind=jnp.bfloat16):
    result = scale * jax.random.normal(stream_key, shape, jnp.float32)
    if split:
        result = result * shard_levels(stream_key, shape, split, -0.22, 0.18)
    return jnp.clip(result, -most, most).astype(kind)


def setup_inputs(seed: int = 0, part: int = 0) -> dict:
    splits = jax.random.split(jax.random.key(seed), 7)
    part_keys = jax.random.split(jax.random.fold_in(splits[6], part), 7)
    return {
        "sens": normal_values(part_keys[0], (2, ND, NC), NC ** -0.5, 0.03125, ((1, 2), (2, 8)), jnp.float32),
        "observed": normal_values(part_keys[1], (2, ND), 1.0, 6.0, ((1, 2),), jnp.float32),
        "noise": jnp.clip(jnp.exp(math.log(2.0) - 1.3862944 * jax.random.uniform(part_keys[2], (2, ND), jnp.float32) ** shard_levels(part_keys[2], (2, ND), ((1, 2),), -0.2, 0.2)), 0.5, 2.0),
        "survey_ids": set_ends(jax.random.randint(part_keys[3], (2, ND), 0, NSURV), jax.random.fold_in(part_keys[3], 1), 0, NSURV - 1).astype(jnp.int32),
        "data_perturb": normal_values(part_keys[4], (2, MODELS, ND), 1.0, 6.0, ((2, 2),), jnp.float32),
        "prior": normal_values(part_keys[5], (2, MODELS, NZ, NY * NX), 1.0, 6.0, ((2, 8),), jnp.float32),
    }


nu_value = 4.0
step_size = 0.5
couple_weight = 0.02
prior_weight = 0.1

def forward_diff(field, axis):
    length = field.shape[axis]
    following = jnp.concatenate([lax.slice_in_dim(field, 1, length, axis=axis), jnp.zeros_like(lax.slice_in_dim(field, 0, 1, axis=axis))], axis=axis)
    keep_shape = [1] * field.ndim
    keep_shape[axis] = length
    keeper = (jnp.arange(length) < length - 1).astype(jnp.float32).reshape(keep_shape)
    return ((following - field) * keeper, keeper)

def backward_diff(values, keeper, axis):
    length = values.shape[axis]
    masked = values * keeper
    preceding = jnp.concatenate([jnp.zeros_like(lax.slice_in_dim(masked, 0, 1, axis=axis)), lax.slice_in_dim(masked, 0, length - 1, axis=axis)], axis=axis)
    return preceding - masked

def coupling(fields):
    diffs = []
    keepers = []
    for axis in (4, 3, 2):
        change, keeper = forward_diff(fields, axis)
        diffs.append(change)
        keepers.append(keeper)
    first = [change[0] for change in diffs]
    second = [change[1] for change in diffs]
    cross_x = first[1] * second[2] - first[2] * second[1]
    cross_y = first[2] * second[0] - first[0] * second[2]
    cross_z = first[0] * second[1] - first[1] * second[0]
    scaling = 2.0 / (1.0 + cross_x * cross_x + cross_y * cross_y + cross_z * cross_z)
    grad_first = [scaling * (second[1] * cross_z - second[2] * cross_y), scaling * (second[2] * cross_x - second[0] * cross_z), scaling * (second[0] * cross_y - second[1] * cross_x)]
    grad_second = [scaling * (cross_y * first[2] - cross_z * first[1]), scaling * (cross_z * first[0] - cross_x * first[2]), scaling * (cross_x * first[1] - cross_y * first[0])]
    total = jnp.zeros_like(fields)
    for index, axis in enumerate((4, 3, 2)):
        stacked = jnp.stack([grad_first[index], grad_second[index]])
        total = total + backward_diff(stacked, keepers[index], axis)
    return total

def reference(sens, observed, noise, survey_ids, data_perturb, prior):
    highest = lax.Precision.HIGHEST
    targets = observed[:, None, :] + noise[:, None, :] * data_perturb
    labels = jnp.arange(NSURV, dtype=jnp.int32)
    one_hot = (survey_ids[:, :, None] == labels).astype(jnp.float32)
    counts = lax.optimization_barrier(jnp.sum(one_hot, axis=1))
    models = prior
    for iteration in range(ITERS):
        flattened = models.reshape(2, MODELS, NZ * NY * NX)
        predicted = jnp.einsum('skc,snc->skn', flattened, sens, precision=highest)
        resid = (predicted - targets) / noise[:, None, :]
        sums = jnp.einsum('skn,snj->skj', resid * resid, one_hot, precision=highest)
        spread = (sums + 1.0) / (counts[:, None, :] + 1.0)
        spread_rows = jnp.einsum('skj,snj->skn', spread, one_hot, precision=highest)
        scale_rows = jnp.sqrt(spread_rows)
        whitened = resid / scale_rows
        factor = (nu_value + 1.0) / (nu_value + whitened * whitened) * whitened / (noise[:, None, :] * scale_rows)
        gradient = jnp.einsum('skn,snc->skc', factor, sens, precision=highest).reshape(2, MODELS, NZ, NY * NX)
        grid_field = models.reshape(2, MODELS, NZ, NY, NX)
        couple = coupling(grid_field).reshape(2, MODELS, NZ, NY * NX)
        models = models - step_size * (gradient + couple_weight * couple + prior_weight * (models - prior))
    return models
```

```python
import functools

import jax
import jax.numpy as jnp
from jax import lax
from jax.experimental import pallas as pl
from jax.experimental.pallas import tpu as pltpu
from jax.sharding import PartitionSpec as P

NX = 32
NSURV = 8
ITERS = 4

nu_value = 4.0
step_size = 0.5
couple_weight = 0.02
prior_weight = 0.1

LANES = 128
MIB = 2**20
BF16 = jnp.bfloat16
F32 = jnp.float32
IN_VMEM = pl.BlockSpec(memory_space=pltpu.VMEM)
IN_HBM = pl.BlockSpec(memory_space=pltpu.HBM)


def dot(left, right):
    return lax.dot_general(
        left, right, (((1,), (0,)), ((), ())), preferred_element_type=F32
    )


def split_rows(values):
    high = values.astype(BF16).astype(F32)
    return jnp.concatenate([high, values - high], axis=0).astype(BF16)


def fold_rows(values):
    half = values.shape[0] // 2
    return values[:half] + values[half:]


def prepare_kernel(
    chunk,
    sens_ref,
    models_ref,
    ids_ref,
    high_ref,
    low_ref,
    high_t_ref,
    low_t_ref,
    part_ref,
    count_ref,
    buffers,
    semaphores,
):
    surveys, stations, cells = sens_ref.shape
    model_count = models_ref.shape[1]
    per_survey = cells // chunk
    total = surveys * per_survey
    slots = buffers.shape[0]

    def copy(step):
        survey = step // per_survey
        start = pl.multiple_of((step % per_survey) * chunk, chunk)
        slot = step % slots
        return pltpu.make_async_copy(
            sens_ref.at[survey, :, pl.ds(start, chunk)],
            buffers.at[slot],
            semaphores.at[slot],
        )

    for step in range(min(slots - 1, total)):
        copy(step).start()
    part_ref[...] = jnp.zeros_like(part_ref)
    lane = lax.broadcasted_iota(jnp.int32, (model_count, LANES), 1)
    for survey in range(surveys):
        ids = jnp.broadcast_to(ids_ref[survey], (model_count, stations))
        counts = jnp.zeros((model_count, LANES), F32)
        for label in range(NSURV):
            here = jnp.sum((ids == label).astype(F32), axis=1, keepdims=True)
            counts = jnp.where(lane == NSURV + label, here, counts)
        count_ref[survey] = counts

    def step_fn(step, carry):
        copy(step).wait()

        @pl.when(step + slots - 1 < total)
        def _():
            copy(step + slots - 1).start()

        survey = step // per_survey
        place = pl.ds(pl.multiple_of((step % per_survey) * chunk, chunk), chunk)
        values = buffers[step % slots]
        high = values.astype(BF16)
        high_ref[survey, :, place] = high
        low_ref[survey, :, place] = (values - high.astype(F32)).astype(BF16)
        turned = values.T
        high_t = turned.astype(BF16)
        low_t = (turned - high_t.astype(F32)).astype(BF16)
        high_t_ref[survey, place, :] = high_t
        low_t_ref[survey, place, :] = low_t
        rows = split_rows(models_ref[survey, :, place])
        part_ref[survey] += fold_rows(dot(rows, high_t) + dot(rows, low_t))
        return carry

    lax.fori_loop(0, total, step_fn, 0)


def prepare(sens, models, ids):
    surveys, stations, cells = sens.shape
    model_count = models.shape[1]
    chunk = min(cells, 512)
    slots = 4
    return pl.pallas_call(
        functools.partial(prepare_kernel, chunk),
        out_shape=[
            pltpu.VMEM((surveys, stations, cells), BF16),
            pltpu.VMEM((surveys, stations, cells), BF16),
            pltpu.VMEM((surveys, cells, stations), BF16),
            pltpu.VMEM((surveys, cells, stations), BF16),
            jax.ShapeDtypeStruct((surveys, model_count, stations), F32),
            jax.ShapeDtypeStruct((surveys, model_count, LANES), F32),
        ],
        in_specs=[IN_HBM, IN_VMEM, IN_VMEM],
        out_specs=[IN_VMEM] * 6,
        scratch_shapes=[
            pltpu.VMEM((slots, stations, chunk), F32),
            pltpu.SemaphoreType.DMA((slots,)),
        ],
        compiler_params=pltpu.CompilerParams(vmem_limit_bytes=16 * MIB),
        name="prepare",
    )(pltpu.with_memory_space_constraint(sens, pltpu.HBM), models, ids)


def stepped(models, prior, own, other):
    return models - step_size * ((own + other) + prior_weight * (models - prior))


def forward_kernel(
    layer_cells,
    models_ref,
    prior_ref,
    own_ref,
    other_ref,
    high_t_ref,
    low_t_ref,
    next_ref,
    edge_ref,
    part_ref,
):
    surveys, _, cells = models_ref.shape
    upward = lax.axis_index("dp") == 0
    for survey in range(surveys):
        models = stepped(
            models_ref[survey], prior_ref[survey], own_ref[survey], other_ref[survey]
        )
        next_ref[survey] = models
        edge_ref[survey] = jnp.where(
            upward, models[:, :layer_cells], models[:, cells - layer_cells :]
        )
        rows = split_rows(models)
        part_ref[survey] = fold_rows(
            dot(rows, high_t_ref[survey]) + dot(rows, low_t_ref[survey])
        )


def forward(models, prior, own, other, high_t, low_t, layer_cells):
    surveys, model_count, _ = models.shape
    stations = high_t.shape[2]
    return pl.pallas_call(
        functools.partial(forward_kernel, layer_cells),
        out_shape=[
            jax.ShapeDtypeStruct(models.shape, F32),
            jax.ShapeDtypeStruct((surveys, model_count, layer_cells), F32),
            jax.ShapeDtypeStruct((surveys, model_count, stations), F32),
        ],
        in_specs=[IN_VMEM] * 6,
        out_specs=[IN_VMEM] * 3,
        compiler_params=pltpu.CompilerParams(vmem_limit_bytes=8 * MIB),
        name="forward",
    )(models, prior, own, other, high_t, low_t)


def cross_terms(field, above, keep_x, keep_y, keep_z, depth_only):
    cells = field[0].shape[1]
    first = []
    second = []
    for grads, here, deeper in zip((first, second), field, above):
        grads.append((pltpu.roll(here, cells - 1, 1) - here) * keep_x)
        grads.append((pltpu.roll(here, cells - NX, 1) - here) * keep_y)
        change = deeper - here
        grads.append(change if keep_z is None else change * keep_z)
    cross_x = first[1] * second[2] - first[2] * second[1]
    cross_y = first[2] * second[0] - first[0] * second[2]
    cross_z = first[0] * second[1] - first[1] * second[0]
    scaling = (2.0 * couple_weight) / (
        1.0 + cross_x * cross_x + cross_y * cross_y + cross_z * cross_z
    )
    depth = [
        scaling * (second[0] * cross_y - second[1] * cross_x),
        scaling * (cross_x * first[1] - cross_y * first[0]),
    ]
    if keep_z is not None:
        depth = [value * keep_z for value in depth]
    if depth_only:
        return depth, None
    grad_x = [
        scaling * (second[1] * cross_z - second[2] * cross_y) * keep_x,
        scaling * (cross_y * first[2] - cross_z * first[1]) * keep_x,
    ]
    grad_y = [
        scaling * (second[2] * cross_x - second[0] * cross_z) * keep_y,
        scaling * (cross_z * first[0] - cross_x * first[2]) * keep_y,
    ]
    level = [
        (pltpu.roll(along_x, 1, 1) - along_x) + (pltpu.roll(along_y, NX, 1) - along_y)
        for along_x, along_y in zip(grad_x, grad_y)
    ]
    return depth, level


def couple_kernel(layer_cells, models_ref, edge_ref, out_ref):
    _, model_count, cells = models_ref.shape
    layers = cells // layer_cells
    middle = layers // 2
    place = lax.broadcasted_iota(jnp.int32, (model_count, layer_cells), 1)
    keep_x = (place % NX < NX - 1).astype(F32)
    keep_y = (place < layer_cells - NX).astype(F32)
    side = lax.axis_index("dp")
    index = lax.axis_index("cell")

    def layer(at):
        if 0 <= at < layers:
            return [
                models_ref[survey, :, at * layer_cells : (at + 1) * layer_cells]
                for survey in range(2)
            ]
        return [edge_ref[survey] for survey in range(2)]

    def write(start, stop):
        sums = {}

        def add(at, values):
            if 0 <= at < layers:
                sums[at] = values if at not in sums else [a + b for a, b in zip(sums[at], values)]

        for at in range(start, stop):
            keep_z = None
            if at < 0:
                keep_z = jnp.where(index > 0, 1.0, 0.0).astype(F32)
            elif at == layers - 1:
                keep_z = jnp.where(index < lax.axis_size("cell") - 1, 1.0, 0.0).astype(F32)
            depth, level = cross_terms(layer(at), layer(at + 1), keep_x, keep_y, keep_z, at < 0)
            if level is not None:
                add(at, [value - below for value, below in zip(level, depth)])
            add(at + 1, depth)
        for at in range(layers):
            for survey in range(2):
                spot = slice(at * layer_cells, (at + 1) * layer_cells)
                if at in sums:
                    out_ref[survey, :, spot] = sums[at][survey]
                else:
                    out_ref[survey, :, spot] = jnp.zeros((model_count, layer_cells), F32)

    @pl.when(side == 0)
    def _():
        write(middle, layers)

    @pl.when(side != 0)
    def _():
        write(-1, middle)


def couple_share(models, edge, layer_cells):
    return pl.pallas_call(
        functools.partial(couple_kernel, layer_cells),
        out_shape=jax.ShapeDtypeStruct(models.shape, F32),
        in_specs=[IN_VMEM] * 2,
        out_specs=IN_VMEM,
        compiler_params=pltpu.CompilerParams(vmem_limit_bytes=4 * MIB),
        name="couple",
    )(models, edge)


def residual_kernel(
    here_ref, there_ref, observed_ref, noise_ref, perturb_ref, ids_ref, count_ref, resid_ref, sums_ref
):
    surveys, model_count, stations = here_ref.shape
    lane = lax.broadcasted_iota(jnp.int32, (model_count, LANES), 1)
    for survey in range(surveys):
        noise = noise_ref[survey]
        targets = observed_ref[survey] + noise * perturb_ref[survey]
        resid = ((here_ref[survey] + there_ref[survey]) - targets) / noise
        resid_ref[survey] = resid
        squares = resid * resid
        ids = jnp.broadcast_to(ids_ref[survey], (model_count, stations))
        sums = count_ref[survey]
        for label in range(NSURV):
            here = jnp.sum(jnp.where(ids == label, squares, 0.0), axis=1, keepdims=True)
            sums = jnp.where(lane == label, here, sums)
        sums_ref[survey] = sums


def residual(here, there, observed, noise, perturb, ids, counts):
    return pl.pallas_call(
        residual_kernel,
        out_shape=[
            jax.ShapeDtypeStruct(here.shape, F32),
            jax.ShapeDtypeStruct(counts.shape, F32),
        ],
        in_specs=[IN_VMEM] * 7,
        out_specs=[IN_VMEM] * 2,
        compiler_params=pltpu.CompilerParams(vmem_limit_bytes=4 * MIB),
        name="residual",
    )(here, there, observed, noise, perturb, ids, counts)


def backward_kernel(
    resid_ref, own_ref, other_ref, noise_ref, ids_ref, couple_ref, high_ref, low_ref, out_ref
):
    surveys, model_count, stations = resid_ref.shape
    for survey in range(surveys):
        sums = own_ref[survey] + other_ref[survey]
        counts = pltpu.roll(sums, LANES - NSURV, 1)
        spread = (sums + 1.0) / (counts + 1.0)
        ids = jnp.broadcast_to(ids_ref[survey], (model_count, stations))
        spread_rows = jnp.zeros((model_count, stations), F32)
        for label in range(NSURV):
            spread_rows = jnp.where(ids == label, spread[:, label : label + 1], spread_rows)
        resid = resid_ref[survey]
        factor = (nu_value + 1.0) * resid / (
            noise_ref[survey] * (nu_value * spread_rows + resid * resid)
        )
        rows = split_rows(factor)
        out_ref[survey] = couple_ref[survey] + fold_rows(
            dot(rows, high_ref[survey]) + dot(rows, low_ref[survey])
        )


def backward(resid, own, other, noise, ids, couple, high, low):
    return pl.pallas_call(
        backward_kernel,
        out_shape=jax.ShapeDtypeStruct(couple.shape, F32),
        in_specs=[IN_VMEM] * 8,
        out_specs=IN_VMEM,
        compiler_params=pltpu.CompilerParams(vmem_limit_bytes=8 * MIB),
        name="backward",
    )(resid, own, other, noise, ids, couple, high, low)


def from_pair(values):
    return lax.ppermute(values, "dp", [(0, 1), (1, 0)])


def exchange_edges(edge):
    devices = lax.axis_size("cell")
    pairs = [(2 * i, 2 * i - 2) for i in range(1, devices)]
    pairs += [(2 * i + 1, 2 * i + 3) for i in range(devices - 1)]
    return lax.ppermute(edge, ("cell", "dp"), pairs)


def fetch(values, by, devices):
    return lax.ppermute(values, "cell", [(i, i ^ by) for i in range(devices)])


def cell_pair(values):
    devices = lax.axis_size("cell")
    stride = devices
    while stride > 2:
        base = 4 if stride >= 8 else 2
        stride //= base
        total = values
        for count in range(1, base):
            total = total + fetch(values, count * stride, devices)
        values = total
    return values, fetch(values, 1, devices)


def body(sens, observed, noise, survey_ids, data_perturb, prior):
    surveys, model_count, layers, layer_cells = prior.shape
    flat = prior.reshape(surveys, model_count, layers * layer_cells)
    observed = observed[:, None, :]
    noise = noise[:, None, :]
    ids = survey_ids[:, None, :]
    models = flat
    edge = jnp.where(
        lax.axis_index("dp") == 0, flat[:, :, :layer_cells], flat[:, :, -layer_cells:]
    )
    edge = exchange_edges(edge)
    high, low, high_t, low_t, part, counts = prepare(sens, flat, ids)
    for iteration in range(ITERS):
        if iteration:
            models, edge, part = forward(models, flat, own, other, high_t, low_t, layer_cells)
            edge = exchange_edges(edge)
        here, there = cell_pair(part)
        couple = couple_share(models, edge, layer_cells)
        resid, own_sums = residual(here, there, observed, noise, data_perturb, ids, counts)
        other_sums = from_pair(own_sums)
        own = backward(resid, own_sums, other_sums, noise, ids, couple, high, low)
        other = from_pair(own)
    models = stepped(models, flat, own, other)
    return models.reshape(prior.shape)


def solution(mesh):
    return jax.shard_map(
        body,
        mesh=mesh,
        in_specs=(
            P(None, ("slab", "dp"), "cell"),
            P(None, ("slab", "dp")),
            P(None, ("slab", "dp")),
            P(None, ("slab", "dp")),
            P(None, None, ("slab", "dp")),
            P(None, "slab", "cell", None),
        ),
        out_specs=P(None, "slab", "cell", None),
        check_vma=False,
    )
```

```python
import functools

import jax
import jax.numpy as jnp
from jax import lax
from jax.experimental import pallas as pl
from jax.experimental.pallas import tpu as pltpu
from jax.sharding import PartitionSpec as P

NX = 32
NSURV = 8
ITERS = 4

nu_value = 4.0
step_size = 0.5
couple_weight = 0.02
prior_weight = 0.1

LANES = 128
MIB = 2**20
BF16 = jnp.bfloat16
F32 = jnp.float32
IN_VMEM = pl.BlockSpec(memory_space=pltpu.VMEM)
IN_HBM = pl.BlockSpec(memory_space=pltpu.HBM)


def dot(left, right):
    return lax.dot_general(
        left, right, (((1,), (0,)), ((), ())), preferred_element_type=F32
    )


def resident(values):
    return pltpu.with_memory_space_constraint(values, pltpu.VMEM)


def split_rows(values):
    high = values.astype(BF16).astype(F32)
    return jnp.concatenate([high, values - high], axis=0).astype(BF16)


def fold_rows(values):
    half = values.shape[0] // 2
    return values[:half] + values[half:]


def flatten_kernel(prior_ref, flat_ref, edge_ref):
    surveys, _, layers, layer_cells = prior_ref.shape
    upward = lax.axis_index("dp") == 0
    for survey in range(surveys):
        rows = [prior_ref[survey, :, at, :] for at in range(layers)]
        for at in range(layers):
            flat_ref[survey, :, at * layer_cells : (at + 1) * layer_cells] = rows[at]
        edge_ref[survey] = jnp.where(upward, rows[0], rows[-1])


def flatten(prior):
    surveys, model_count, layers, layer_cells = prior.shape
    return pl.pallas_call(
        flatten_kernel,
        out_shape=[
            jax.ShapeDtypeStruct((surveys, model_count, layers * layer_cells), F32),
            jax.ShapeDtypeStruct((surveys, model_count, layer_cells), F32),
        ],
        in_specs=[IN_VMEM],
        out_specs=[IN_VMEM] * 2,
        compiler_params=pltpu.CompilerParams(vmem_limit_bytes=4 * MIB),
        name="flatten",
    )(prior)


def finish_kernel(models_ref, prior_ref, own_ref, other_ref, out_ref):
    surveys, _, layers, layer_cells = out_ref.shape
    for survey in range(surveys):
        for at in range(layers):
            spot = slice(at * layer_cells, (at + 1) * layer_cells)
            out_ref[survey, :, at, :] = stepped(
                models_ref[survey, :, spot],
                prior_ref[survey, :, spot],
                own_ref[survey, :, spot],
                other_ref[survey, :, spot],
            )


def finish(models, prior, own, other, shape):
    return pl.pallas_call(
        finish_kernel,
        out_shape=jax.ShapeDtypeStruct(shape, F32),
        in_specs=[IN_VMEM] * 4,
        out_specs=IN_VMEM,
        compiler_params=pltpu.CompilerParams(vmem_limit_bytes=4 * MIB),
        name="finish",
    )(models, prior, own, other)


def prepare_kernel(
    chunk,
    sens_ref,
    models_ref,
    ids_ref,
    split_ref,
    turned_ref,
    part_ref,
    count_ref,
    buffers,
    semaphores,
):
    surveys, stations, cells = sens_ref.shape
    model_count = models_ref.shape[1]
    per_survey = cells // chunk
    total = surveys * per_survey
    slots = buffers.shape[0]

    def copy(step):
        survey = step // per_survey
        start = pl.multiple_of((step % per_survey) * chunk, chunk)
        slot = step % slots
        return pltpu.make_async_copy(
            sens_ref.at[survey, :, pl.ds(start, chunk)],
            buffers.at[slot],
            semaphores.at[slot],
        )

    for step in range(min(slots - 1, total)):
        copy(step).start()
    part_ref[...] = jnp.zeros_like(part_ref)
    lane = lax.broadcasted_iota(jnp.int32, (model_count, LANES), 1)
    for survey in range(surveys):
        ids = jnp.broadcast_to(ids_ref[survey : survey + 1], (model_count, stations))
        counts = jnp.zeros((model_count, LANES), F32)
        for label in range(NSURV):
            here = jnp.sum((ids == label).astype(F32), axis=1, keepdims=True)
            counts = jnp.where(lane == NSURV + label, here, counts)
        count_ref[survey] = counts

    def step_fn(step, carry):
        copy(step).wait()

        @pl.when(step + slots - 1 < total)
        def _():
            copy(step + slots - 1).start()

        survey = step // per_survey
        place = pl.ds(pl.multiple_of((step % per_survey) * chunk, chunk), chunk)
        values = buffers[step % slots]
        high = values.astype(BF16)
        split_ref[0, survey, :, place] = high
        split_ref[1, survey, :, place] = (values - high.astype(F32)).astype(BF16)
        turned = values.T
        high_t = turned.astype(BF16)
        low_t = (turned - high_t.astype(F32)).astype(BF16)
        turned_ref[0, survey, place, :] = high_t
        turned_ref[1, survey, place, :] = low_t
        rows = split_rows(models_ref[survey, :, place])
        part_ref[survey] += fold_rows(dot(rows, high_t) + dot(rows, low_t))
        return carry

    lax.fori_loop(0, total, step_fn, 0)


def prepare(sens, models, ids):
    surveys, stations, cells = sens.shape
    model_count = models.shape[1]
    chunk = min(cells, 512)
    slots = 4
    return pl.pallas_call(
        functools.partial(prepare_kernel, chunk),
        out_shape=[
            pltpu.VMEM((2, surveys, stations, cells), BF16),
            pltpu.VMEM((2, surveys, cells, stations), BF16),
            jax.ShapeDtypeStruct((surveys, model_count, stations), F32),
            jax.ShapeDtypeStruct((surveys, model_count, LANES), F32),
        ],
        in_specs=[IN_HBM, IN_VMEM, IN_VMEM],
        out_specs=[IN_VMEM] * 4,
        scratch_shapes=[
            pltpu.VMEM((slots, stations, chunk), F32),
            pltpu.SemaphoreType.DMA((slots,)),
        ],
        compiler_params=pltpu.CompilerParams(vmem_limit_bytes=9 * MIB),
        name="prepare",
    )(pltpu.with_memory_space_constraint(sens, pltpu.HBM), models, ids)


def stepped(models, prior, own, other):
    return models - step_size * ((own + other) + prior_weight * (models - prior))


def forward_kernel(
    layer_cells,
    models_ref,
    prior_ref,
    own_ref,
    other_ref,
    turned_ref,
    next_ref,
    edge_ref,
    part_ref,
):
    surveys, _, cells = models_ref.shape
    upward = lax.axis_index("dp") == 0
    for survey in range(surveys):
        models = stepped(
            models_ref[survey], prior_ref[survey], own_ref[survey], other_ref[survey]
        )
        next_ref[survey] = models
        edge_ref[survey] = jnp.where(
            upward, models[:, :layer_cells], models[:, cells - layer_cells :]
        )
        rows = split_rows(models)
        part_ref[survey] = fold_rows(
            dot(rows, turned_ref[0, survey]) + dot(rows, turned_ref[1, survey])
        )


def forward(models, prior, own, other, turned, layer_cells):
    surveys, model_count, _ = models.shape
    stations = turned.shape[3]
    return pl.pallas_call(
        functools.partial(forward_kernel, layer_cells),
        out_shape=[
            jax.ShapeDtypeStruct(models.shape, F32),
            jax.ShapeDtypeStruct((surveys, model_count, layer_cells), F32),
            jax.ShapeDtypeStruct((surveys, model_count, stations), F32),
        ],
        in_specs=[IN_VMEM] * 5,
        out_specs=[IN_VMEM] * 3,
        compiler_params=pltpu.CompilerParams(vmem_limit_bytes=4 * MIB),
        name="forward",
    )(models, prior, own, other, resident(turned))


def cross_terms(field, above, keep_x, keep_y, keep_z, depth_only):
    cells = field[0].shape[1]
    first = []
    second = []
    for grads, here, deeper in zip((first, second), field, above):
        grads.append((pltpu.roll(here, cells - 1, 1) - here) * keep_x)
        grads.append((pltpu.roll(here, cells - NX, 1) - here) * keep_y)
        change = deeper - here
        grads.append(change if keep_z is None else change * keep_z)
    cross_x = first[1] * second[2] - first[2] * second[1]
    cross_y = first[2] * second[0] - first[0] * second[2]
    cross_z = first[0] * second[1] - first[1] * second[0]
    scaling = (2.0 * couple_weight) / (
        1.0 + cross_x * cross_x + cross_y * cross_y + cross_z * cross_z
    )
    depth = [
        scaling * (second[0] * cross_y - second[1] * cross_x),
        scaling * (cross_x * first[1] - cross_y * first[0]),
    ]
    if keep_z is not None:
        depth = [value * keep_z for value in depth]
    if depth_only:
        return depth, None
    grad_x = [
        scaling * (second[1] * cross_z - second[2] * cross_y) * keep_x,
        scaling * (cross_y * first[2] - cross_z * first[1]) * keep_x,
    ]
    grad_y = [
        scaling * (second[2] * cross_x - second[0] * cross_z) * keep_y,
        scaling * (cross_z * first[0] - cross_x * first[2]) * keep_y,
    ]
    level = [
        (pltpu.roll(along_x, 1, 1) - along_x) + (pltpu.roll(along_y, NX, 1) - along_y)
        for along_x, along_y in zip(grad_x, grad_y)
    ]
    return depth, level


def couple_kernel(layer_cells, models_ref, edge_ref, out_ref):
    _, model_count, cells = models_ref.shape
    layers = cells // layer_cells
    middle = layers // 2
    place = lax.broadcasted_iota(jnp.int32, (model_count, layer_cells), 1)
    keep_x = (place % NX < NX - 1).astype(F32)
    keep_y = (place < layer_cells - NX).astype(F32)
    side = lax.axis_index("dp")
    index = lax.axis_index("cell")

    def layer(at):
        if 0 <= at < layers:
            return [
                models_ref[survey, :, at * layer_cells : (at + 1) * layer_cells]
                for survey in range(2)
            ]
        return [edge_ref[survey] for survey in range(2)]

    def write(start, stop):
        sums = {}

        def add(at, values):
            if 0 <= at < layers:
                sums[at] = values if at not in sums else [a + b for a, b in zip(sums[at], values)]

        for at in range(start, stop):
            keep_z = None
            if at < 0:
                keep_z = jnp.where(index > 0, 1.0, 0.0).astype(F32)
            elif at == layers - 1:
                keep_z = jnp.where(index < lax.axis_size("cell") - 1, 1.0, 0.0).astype(F32)
            depth, level = cross_terms(layer(at), layer(at + 1), keep_x, keep_y, keep_z, at < 0)
            if level is not None:
                add(at, [value - below for value, below in zip(level, depth)])
            add(at + 1, depth)
        for at in range(layers):
            for survey in range(2):
                spot = slice(at * layer_cells, (at + 1) * layer_cells)
                if at in sums:
                    out_ref[survey, :, spot] = sums[at][survey]
                else:
                    out_ref[survey, :, spot] = jnp.zeros((model_count, layer_cells), F32)

    @pl.when(side == 0)
    def _():
        write(middle, layers)

    @pl.when(side != 0)
    def _():
        write(-1, middle)


def couple_share(models, edge, layer_cells):
    return pl.pallas_call(
        functools.partial(couple_kernel, layer_cells),
        out_shape=jax.ShapeDtypeStruct(models.shape, F32),
        in_specs=[IN_VMEM] * 2,
        out_specs=IN_VMEM,
        compiler_params=pltpu.CompilerParams(vmem_limit_bytes=4 * MIB),
        name="couple",
    )(models, edge)


def residual_kernel(
    here_ref, there_ref, observed_ref, noise_ref, perturb_ref, ids_ref, count_ref, resid_ref, sums_ref
):
    surveys, model_count, stations = here_ref.shape
    lane = lax.broadcasted_iota(jnp.int32, (model_count, LANES), 1)
    for survey in range(surveys):
        noise = noise_ref[survey : survey + 1]
        targets = observed_ref[survey : survey + 1] + noise * perturb_ref[survey]
        resid = ((here_ref[survey] + there_ref[survey]) - targets) / noise
        resid_ref[survey] = resid
        squares = resid * resid
        ids = jnp.broadcast_to(ids_ref[survey : survey + 1], (model_count, stations))
        sums = count_ref[survey]
        for label in range(NSURV):
            here = jnp.sum(jnp.where(ids == label, squares, 0.0), axis=1, keepdims=True)
            sums = jnp.where(lane == label, here, sums)
        sums_ref[survey] = sums


def residual(here, there, observed, noise, perturb, ids, counts):
    return pl.pallas_call(
        residual_kernel,
        out_shape=[
            jax.ShapeDtypeStruct(here.shape, F32),
            jax.ShapeDtypeStruct(counts.shape, F32),
        ],
        in_specs=[IN_VMEM] * 7,
        out_specs=[IN_VMEM] * 2,
        compiler_params=pltpu.CompilerParams(vmem_limit_bytes=4 * MIB),
        name="residual",
    )(here, there, observed, noise, perturb, ids, counts)


def backward_kernel(
    resid_ref, own_ref, other_ref, noise_ref, ids_ref, couple_ref, split_ref, out_ref
):
    surveys, model_count, stations = resid_ref.shape
    for survey in range(surveys):
        sums = own_ref[survey] + other_ref[survey]
        counts = pltpu.roll(sums, LANES - NSURV, 1)
        spread = (sums + 1.0) / (counts + 1.0)
        ids = jnp.broadcast_to(ids_ref[survey : survey + 1], (model_count, stations))
        spread_rows = jnp.zeros((model_count, stations), F32)
        for label in range(NSURV):
            spread_rows = jnp.where(ids == label, spread[:, label : label + 1], spread_rows)
        resid = resid_ref[survey]
        factor = (nu_value + 1.0) * resid / (
            noise_ref[survey : survey + 1] * (nu_value * spread_rows + resid * resid)
        )
        rows = split_rows(factor)
        out_ref[survey] = couple_ref[survey] + fold_rows(
            dot(rows, split_ref[0, survey]) + dot(rows, split_ref[1, survey])
        )


def backward(resid, own, other, noise, ids, couple, split):
    return pl.pallas_call(
        backward_kernel,
        out_shape=jax.ShapeDtypeStruct(couple.shape, F32),
        in_specs=[IN_VMEM] * 7,
        out_specs=IN_VMEM,
        compiler_params=pltpu.CompilerParams(vmem_limit_bytes=4 * MIB),
        name="backward",
    )(resid, own, other, noise, ids, couple, resident(split))


def from_pair(values):
    return lax.ppermute(values, "dp", [(0, 1), (1, 0)])


def exchange_edges(edge):
    devices = lax.axis_size("cell")
    pairs = [(2 * i, 2 * i - 2) for i in range(1, devices)]
    pairs += [(2 * i + 1, 2 * i + 3) for i in range(devices - 1)]
    return lax.ppermute(edge, ("cell", "dp"), pairs)


def fetch(values, by, devices):
    return lax.ppermute(values, "cell", [(i, i ^ by) for i in range(devices)])


def cell_pair(values):
    devices = lax.axis_size("cell")
    stride = devices
    while stride > 2:
        base = 4 if stride >= 8 else 2
        stride //= base
        total = values
        for count in range(1, base):
            total = total + fetch(values, count * stride, devices)
        values = total
    return values, fetch(values, 1, devices)


def body(sens, observed, noise, survey_ids, data_perturb, prior):
    layer_cells = prior.shape[3]
    ids = survey_ids
    flat, edge = flatten(prior)
    models = flat
    edge = exchange_edges(edge)
    split, turned, part, counts = prepare(sens, flat, ids)
    for iteration in range(ITERS):
        if iteration:
            models, edge, part = forward(models, flat, own, other, turned, layer_cells)
            edge = exchange_edges(edge)
        here, there = cell_pair(part)
        couple = couple_share(models, edge, layer_cells)
        resid, own_sums = residual(here, there, observed, noise, data_perturb, ids, counts)
        other_sums = from_pair(own_sums)
        own = backward(resid, own_sums, other_sums, noise, ids, couple, split)
        other = from_pair(own)
    return finish(models, flat, own, other, prior.shape)


def solution(mesh):
    return jax.shard_map(
        body,
        mesh=mesh,
        in_specs=(
            P(None, ("slab", "dp"), "cell"),
            P(None, ("slab", "dp")),
            P(None, ("slab", "dp")),
            P(None, ("slab", "dp")),
            P(None, None, ("slab", "dp")),
            P(None, "slab", "cell", None),
        ),
        out_specs=P(None, "slab", "cell", None),
        check_vma=False,
    )
```

```python
import functools

import jax
import jax.numpy as jnp
from jax import lax
from jax.experimental import pallas as pl
from jax.experimental.pallas import tpu as pltpu
from jax.sharding import PartitionSpec as P

NX = 32
NSURV = 8
ITERS = 4

nu_value = 4.0
step_size = 0.5
couple_weight = 0.02
prior_weight = 0.1

LANES = 128
MIB = 2**20
BF16 = jnp.bfloat16
F32 = jnp.float32
IN_VMEM = pl.BlockSpec(memory_space=pltpu.VMEM)
IN_HBM = pl.BlockSpec(memory_space=pltpu.HBM)


def dot(left, right, along=0):
    return lax.dot_general(
        left, right, (((1,), (along,)), ((), ())), preferred_element_type=F32
    )


def resident(values):
    return pltpu.with_memory_space_constraint(values, pltpu.VMEM)


def split_rows(values):
    high = values.astype(BF16).astype(F32)
    return jnp.concatenate([high, values - high], axis=0).astype(BF16)


def fold_rows(values):
    half = values.shape[0] // 2
    return values[:half] + values[half:]


def prepare_kernel(
    block,
    sens_ref,
    prior_ref,
    ids_ref,
    split_ref,
    turned_ref,
    part_ref,
    count_ref,
    edge_ref,
    *rest,
):
    surveys, stations, _ = sens_ref.shape
    _, model_count, layers, layer_cells = prior_ref.shape
    flat_refs = rest[:surveys]
    buffers, prior_buffer, ids_buffer, semaphores, small_semaphores = rest[surveys:]
    per_survey = stations // block
    total = surveys * per_survey
    slots = buffers.shape[0]

    def copy(step):
        start = pl.multiple_of((step % per_survey) * block, block)
        slot = step % slots
        return pltpu.make_async_copy(
            sens_ref.at[step // per_survey, pl.ds(start, block), :],
            buffers.at[slot],
            semaphores.at[slot],
        )

    prior_copy = pltpu.make_async_copy(prior_ref, prior_buffer, small_semaphores.at[0])
    ids_copy = pltpu.make_async_copy(ids_ref, ids_buffer, small_semaphores.at[1])
    prior_copy.start()
    for step in range(min(slots - 1, total)):
        copy(step).start()
    ids_copy.start()
    prior_copy.wait()
    upward = lax.axis_index("dp") == 0
    for survey in range(surveys):
        layer_rows = [prior_buffer[survey, :, at, :] for at in range(layers)]
        for at in range(layers):
            flat_refs[survey][:, at * layer_cells : (at + 1) * layer_cells] = layer_rows[at]
        edge_ref[survey] = jnp.where(upward, layer_rows[0], layer_rows[-1])
    ids_copy.wait()
    lane = lax.broadcasted_iota(jnp.int32, (model_count, LANES), 1)
    for survey in range(surveys):
        ids = jnp.broadcast_to(ids_buffer[survey : survey + 1], (model_count, stations))
        counts = jnp.zeros((model_count, LANES), F32)
        for label in range(NSURV):
            here = jnp.sum((ids == label).astype(F32), axis=1, keepdims=True)
            counts = jnp.where(lane == NSURV + label, here, counts)
        count_ref[survey] = counts
    for survey in range(surveys):
        rows = split_rows(flat_refs[survey][...])

        def step_fn(at, carry):
            step = survey * per_survey + at
            copy(step).wait()

            @pl.when(step + slots - 1 < total)
            def _():
                copy(step + slots - 1).start()

            place = pl.ds(pl.multiple_of(at * block, block), block)
            values = buffers[step % slots]
            high = values.astype(BF16)
            low = (values - high.astype(F32)).astype(BF16)
            split_ref[0, survey, place, :] = high
            split_ref[1, survey, place, :] = low
            turned = values.T
            high_t = turned.astype(BF16)
            turned_ref[0, survey, :, place] = high_t
            turned_ref[1, survey, :, place] = (turned - high_t.astype(F32)).astype(BF16)
            part_ref[survey, :, place] = fold_rows(dot(rows, high, 1) + dot(rows, low, 1))
            return carry

        lax.fori_loop(0, per_survey, step_fn, 0)


def prepare(sens, prior, ids):
    surveys, stations, cells = sens.shape
    _, model_count, _, layer_cells = prior.shape
    block = min(stations, LANES)
    slots = 5
    outs = pl.pallas_call(
        functools.partial(prepare_kernel, block),
        out_shape=[
            pltpu.VMEM((2, surveys, stations, cells), BF16),
            pltpu.VMEM((2, surveys, cells, stations), BF16),
            jax.ShapeDtypeStruct((surveys, model_count, stations), F32),
            jax.ShapeDtypeStruct((surveys, model_count, LANES), F32),
            jax.ShapeDtypeStruct((surveys, model_count, layer_cells), F32),
        ]
        + [jax.ShapeDtypeStruct((model_count, cells), F32)] * surveys,
        in_specs=[IN_HBM] * 3,
        out_specs=[IN_VMEM] * (5 + surveys),
        scratch_shapes=[
            pltpu.VMEM((slots, block, cells), F32),
            pltpu.VMEM(prior.shape, F32),
            pltpu.VMEM(ids.shape, jnp.int32),
            pltpu.SemaphoreType.DMA((slots,)),
            pltpu.SemaphoreType.DMA((2,)),
        ],
        compiler_params=pltpu.CompilerParams(vmem_limit_bytes=12 * MIB),
        name="prepare",
    )(*[pltpu.with_memory_space_constraint(x, pltpu.HBM) for x in (sens, prior, ids)])
    return *outs[:5], list(outs[5:])


def stepped(models, prior, own, other):
    return models - step_size * ((own + other) + prior_weight * (models - prior))


def forward_kernel(survey, *refs):
    models_ref, prior_ref, own_ref, other_ref, turned_ref = refs[:5]
    models = stepped(models_ref[...], prior_ref[...], own_ref[...], other_ref[...])
    rows = split_rows(models)
    part = fold_rows(dot(rows, turned_ref[0, survey]) + dot(rows, turned_ref[1, survey]))
    refs = refs[5:]
    if survey + 1 < turned_ref.shape[1]:
        next_ref, part_ref = refs
        next_ref[...] = models
        part_ref[...] = part
        return
    earlier_models = refs[:survey]
    earlier_parts = refs[survey : 2 * survey]
    next_ref, edge_ref, part_ref = refs[2 * survey :]
    next_ref[...] = models
    part_ref[survey] = part
    for at in range(survey):
        part_ref[at] = earlier_parts[at][...]
    cells = models.shape[1]
    layer_cells = edge_ref.shape[2]
    upward = lax.axis_index("dp") == 0
    for at, ref in enumerate((*earlier_models, next_ref)):
        edge_ref[at] = jnp.where(
            upward, ref[:, :layer_cells], ref[:, cells - layer_cells :]
        )


def forward(models, prior, owns, others, turned, layer_cells):
    surveys = len(models)
    model_count, _ = models[0].shape
    stations = turned.shape[3]
    moved = []
    parts = []
    for survey in range(surveys):
        out_shape = [jax.ShapeDtypeStruct(models[survey].shape, F32)]
        operands = [models[survey], prior[survey], owns[survey], others[survey], resident(turned)]
        if survey + 1 < surveys:
            out_shape += [jax.ShapeDtypeStruct((model_count, stations), F32)]
        else:
            operands += moved + parts
            out_shape += [
                jax.ShapeDtypeStruct((surveys, model_count, layer_cells), F32),
                jax.ShapeDtypeStruct((surveys, model_count, stations), F32),
            ]
        outs = pl.pallas_call(
            functools.partial(forward_kernel, survey),
            out_shape=out_shape,
            in_specs=[IN_VMEM] * len(operands),
            out_specs=[IN_VMEM] * len(out_shape),
            compiler_params=pltpu.CompilerParams(vmem_limit_bytes=4 * MIB),
            cost_estimate=product_cost(turned),
            name="forward",
        )(*operands)
        moved.append(outs[0])
        parts.append(outs[1])
    return moved, outs[1], outs[2]


def product_cost(split):
    cells = split.shape[2] * split.shape[3]
    return pl.CostEstimate(flops=512 * cells, bytes_accessed=4 * cells, transcendentals=0)


def cross_terms(field, above, keep_x, keep_y, keep_z, depth_only):
    cells = field[0].shape[1]
    first = []
    second = []
    for grads, here, deeper in zip((first, second), field, above):
        grads.append((pltpu.roll(here, cells - 1, 1) - here) * keep_x)
        grads.append((pltpu.roll(here, cells - NX, 1) - here) * keep_y)
        change = deeper - here
        grads.append(change if keep_z is None else change * keep_z)
    cross_x = first[1] * second[2] - first[2] * second[1]
    cross_y = first[2] * second[0] - first[0] * second[2]
    cross_z = first[0] * second[1] - first[1] * second[0]
    scaling = (2.0 * couple_weight) / (
        1.0 + cross_x * cross_x + cross_y * cross_y + cross_z * cross_z
    )
    depth = [
        scaling * (second[0] * cross_y - second[1] * cross_x),
        scaling * (cross_x * first[1] - cross_y * first[0]),
    ]
    if keep_z is not None:
        depth = [value * keep_z for value in depth]
    if depth_only:
        return depth, None
    grad_x = [
        scaling * (second[1] * cross_z - second[2] * cross_y) * keep_x,
        scaling * (cross_y * first[2] - cross_z * first[1]) * keep_x,
    ]
    grad_y = [
        scaling * (second[2] * cross_x - second[0] * cross_z) * keep_y,
        scaling * (cross_z * first[0] - cross_x * first[2]) * keep_y,
    ]
    level = [
        (pltpu.roll(along_x, 1, 1) - along_x) + (pltpu.roll(along_y, NX, 1) - along_y)
        for along_x, along_y in zip(grad_x, grad_y)
    ]
    return depth, level


def couple_kernel(layer_cells, *refs):
    models_refs, edge_ref, out_refs = refs[:2], refs[2], refs[3:]
    model_count, cells = models_refs[0].shape
    layers = cells // layer_cells
    middle = layers // 2
    place = lax.broadcasted_iota(jnp.int32, (model_count, layer_cells), 1)
    keep_x = (place % NX < NX - 1).astype(F32)
    keep_y = (place < layer_cells - NX).astype(F32)
    side = lax.axis_index("dp")
    index = lax.axis_index("cell")

    def layer(at):
        if 0 <= at < layers:
            return [
                ref[:, at * layer_cells : (at + 1) * layer_cells] for ref in models_refs
            ]
        return [edge_ref[survey] for survey in range(2)]

    def write(start, stop):
        sums = {}

        def add(at, values):
            if 0 <= at < layers:
                sums[at] = values if at not in sums else [a + b for a, b in zip(sums[at], values)]

        for at in range(start, stop):
            keep_z = None
            if at < 0:
                keep_z = jnp.where(index > 0, 1.0, 0.0).astype(F32)
            elif at == layers - 1:
                keep_z = jnp.where(index < lax.axis_size("cell") - 1, 1.0, 0.0).astype(F32)
            depth, level = cross_terms(layer(at), layer(at + 1), keep_x, keep_y, keep_z, at < 0)
            if level is not None:
                add(at, [value - below for value, below in zip(level, depth)])
            add(at + 1, depth)
        for at in range(layers):
            for survey in range(2):
                spot = slice(at * layer_cells, (at + 1) * layer_cells)
                if at in sums:
                    out_refs[survey][:, spot] = sums[at][survey]
                else:
                    out_refs[survey][:, spot] = jnp.zeros((model_count, layer_cells), F32)

    @pl.when(side == 0)
    def _():
        write(middle, layers)

    @pl.when(side != 0)
    def _():
        write(-1, middle)


def couple_share(models, edge, layer_cells):
    return pl.pallas_call(
        functools.partial(couple_kernel, layer_cells),
        out_shape=[jax.ShapeDtypeStruct(x.shape, F32) for x in models],
        in_specs=[IN_VMEM] * 3,
        out_specs=[IN_VMEM] * 2,
        compiler_params=pltpu.CompilerParams(vmem_limit_bytes=4 * MIB),
        name="couple",
    )(*models, edge)


def residual_kernel(
    here_ref, there_ref, observed_ref, noise_ref, perturb_ref, ids_ref, count_ref, resid_ref, sums_ref
):
    surveys, model_count, stations = here_ref.shape
    lane = lax.broadcasted_iota(jnp.int32, (model_count, LANES), 1)
    for survey in range(surveys):
        noise = noise_ref[survey : survey + 1]
        targets = observed_ref[survey : survey + 1] + noise * perturb_ref[survey]
        resid = ((here_ref[survey] + there_ref[survey]) - targets) / noise
        resid_ref[survey] = resid
        squares = resid * resid
        ids = jnp.broadcast_to(ids_ref[survey : survey + 1], (model_count, stations))
        sums = count_ref[survey]
        for label in range(NSURV):
            here = jnp.sum(jnp.where(ids == label, squares, 0.0), axis=1, keepdims=True)
            sums = jnp.where(lane == label, here, sums)
        sums_ref[survey] = sums


def residual(here, there, observed, noise, perturb, ids, counts):
    return pl.pallas_call(
        residual_kernel,
        out_shape=[
            jax.ShapeDtypeStruct(here.shape, F32),
            jax.ShapeDtypeStruct(counts.shape, F32),
        ],
        in_specs=[IN_VMEM] * 7,
        out_specs=[IN_VMEM] * 2,
        compiler_params=pltpu.CompilerParams(vmem_limit_bytes=4 * MIB),
        name="residual",
    )(here, there, observed, noise, perturb, ids, counts)


def backward_kernel(
    survey, resid_ref, own_ref, other_ref, noise_ref, ids_ref, couple_ref, split_ref, out_ref
):
    _, model_count, stations = resid_ref.shape
    sums = own_ref[survey] + other_ref[survey]
    counts = pltpu.roll(sums, LANES - NSURV, 1)
    spread = (sums + 1.0) / (counts + 1.0)
    ids = jnp.broadcast_to(ids_ref[survey : survey + 1], (model_count, stations))
    spread_rows = jnp.zeros((model_count, stations), F32)
    for label in range(NSURV):
        spread_rows = jnp.where(ids == label, spread[:, label : label + 1], spread_rows)
    resid = resid_ref[survey]
    factor = (nu_value + 1.0) * resid / (
        noise_ref[survey : survey + 1] * (nu_value * spread_rows + resid * resid)
    )
    rows = split_rows(factor)
    out_ref[...] = couple_ref[...] + fold_rows(
        dot(rows, split_ref[0, survey]) + dot(rows, split_ref[1, survey])
    )


def backward(survey, resid, own, other, noise, ids, couple, split):
    return pl.pallas_call(
        functools.partial(backward_kernel, survey),
        out_shape=jax.ShapeDtypeStruct(couple.shape, F32),
        in_specs=[IN_VMEM] * 7,
        out_specs=IN_VMEM,
        compiler_params=pltpu.CompilerParams(vmem_limit_bytes=4 * MIB),
        cost_estimate=product_cost(split),
        name="backward",
    )(resid, own, other, noise, ids, couple, resident(split))


def step_kernel(models_ref, prior_ref, own_ref, other_ref, next_ref):
    next_ref[...] = stepped(models_ref[...], prior_ref[...], own_ref[...], other_ref[...])


def finish_kernel(*refs):
    out_ref = refs[-1]
    surveys, _, layers, layer_cells = out_ref.shape
    for survey in range(surveys):
        ready = survey + 1 < surveys
        models = refs[survey][...] if ready else stepped(*[ref[...] for ref in refs[survey:-1]])
        for at in range(layers):
            out_ref[survey, :, at, :] = models[:, at * layer_cells : (at + 1) * layer_cells]


def finish(models, prior, owns, others, shape):
    operands = []
    for survey in range(shape[0]):
        mine = [models[survey], prior[survey], owns[survey], others[survey]]
        if survey + 1 < shape[0]:
            mine = [
                pl.pallas_call(
                    step_kernel,
                    out_shape=jax.ShapeDtypeStruct(models[survey].shape, F32),
                    in_specs=[IN_VMEM] * 4,
                    out_specs=IN_VMEM,
                    compiler_params=pltpu.CompilerParams(vmem_limit_bytes=4 * MIB),
                    name="step",
                )(*mine)
            ]
        operands += mine
    return pl.pallas_call(
        finish_kernel,
        out_shape=jax.ShapeDtypeStruct(shape, F32),
        in_specs=[IN_VMEM] * len(operands),
        out_specs=IN_VMEM,
        compiler_params=pltpu.CompilerParams(vmem_limit_bytes=4 * MIB),
        name="finish",
    )(*operands)


def from_pair(values):
    return lax.ppermute(values, "dp", [(0, 1), (1, 0)])


def exchange_edges(edge):
    devices = lax.axis_size("cell")
    pairs = [(2 * i, 2 * i - 2) for i in range(1, devices)]
    pairs += [(2 * i + 1, 2 * i + 3) for i in range(devices - 1)]
    return lax.ppermute(edge, ("cell", "dp"), pairs)


def fetch(values, by, devices):
    return lax.ppermute(values, "cell", [(i, i ^ by) for i in range(devices)])


def cell_pair(values):
    devices = lax.axis_size("cell")
    stride = devices
    while stride > 2:
        base = 4 if stride >= 8 else 2
        stride //= base
        total = values
        for count in range(1, base):
            total = total + fetch(values, count * stride, devices)
        values = total
    return values, fetch(values, 1, devices)


def body(sens, observed, noise, ids, data_perturb, prior):
    surveys, _, _, layer_cells = prior.shape
    split, turned, part, counts, edge, flat = prepare(sens, prior, ids)
    models = flat
    for iteration in range(ITERS):
        if iteration:
            models, edge, part = forward(models, flat, owns, others, turned, layer_cells)
        edge = exchange_edges(edge)
        here, there = cell_pair(part)
        couple = couple_share(models, edge, layer_cells)
        resid, own_sums = residual(here, there, observed, noise, data_perturb, ids, counts)
        other_sums = from_pair(own_sums)
        owns = []
        others = []
        for survey in range(surveys):
            own = backward(
                survey, resid, own_sums, other_sums, noise, ids, couple[survey], split
            )
            owns.append(own)
            others.append(from_pair(own))
    return finish(models, flat, owns, others, prior.shape)


def solution(mesh):
    return jax.shard_map(
        body,
        mesh=mesh,
        in_specs=(
            P(None, ("slab", "dp"), "cell"),
            P(None, ("slab", "dp")),
            P(None, ("slab", "dp")),
            P(None, ("slab", "dp")),
            P(None, None, ("slab", "dp")),
            P(None, "slab", "cell", None),
        ),
        out_specs=P(None, "slab", "cell", None),
        check_vma=False,
    )
```

```python
import functools

import jax
import jax.numpy as jnp
from jax import lax
from jax.experimental import pallas as pl
from jax.experimental.pallas import tpu as pltpu
from jax.sharding import PartitionSpec as P

NX = 32
NSURV = 8
ITERS = 4

nu_value = 4.0
step_size = 0.5
couple_weight = 0.02
prior_weight = 0.1

LANES = 128
MIB = 2**20
BF16 = jnp.bfloat16
F32 = jnp.float32
IN_VMEM = pl.BlockSpec(memory_space=pltpu.VMEM)
IN_HBM = pl.BlockSpec(memory_space=pltpu.HBM)


def dot(left, right, along=0):
    return lax.dot_general(
        left, right, (((1,), (along,)), ((), ())), preferred_element_type=F32
    )


def resident(values):
    return pltpu.with_memory_space_constraint(values, pltpu.VMEM)


def split_rows(values):
    high = values.astype(BF16).astype(F32)
    return jnp.concatenate([high, values - high], axis=0).astype(BF16)


def fold_rows(values):
    half = values.shape[0] // 2
    return values[:half] + values[half:]


def prepare_kernel(
    block,
    sens_ref,
    prior_ref,
    ids_ref,
    split_ref,
    turned_ref,
    part_ref,
    count_ref,
    edge_ref,
    *rest,
):
    surveys, stations, _ = sens_ref.shape
    _, model_count, layers, layer_cells = prior_ref.shape
    flat_refs = rest[:surveys]
    buffers, prior_buffer, ids_buffer, semaphores, small_semaphores = rest[surveys:]
    per_survey = stations // block
    total = surveys * per_survey
    slots = buffers.shape[0]

    def copy(step):
        start = pl.multiple_of((step % per_survey) * block, block)
        slot = step % slots
        return pltpu.make_async_copy(
            sens_ref.at[step // per_survey, pl.ds(start, block), :],
            buffers.at[slot],
            semaphores.at[slot],
        )

    prior_copy = pltpu.make_async_copy(prior_ref, prior_buffer, small_semaphores.at[0])
    ids_copy = pltpu.make_async_copy(ids_ref, ids_buffer, small_semaphores.at[1])
    ahead = min(slots - 1, total)
    prior_copy.start()
    ids_copy.start()
    for step in range(min(2, ahead)):
        copy(step).start()
    prior_copy.wait()
    for step in range(min(2, ahead), ahead):
        copy(step).start()
    upward = lax.axis_index("dp") == 0
    for survey in range(surveys):
        layer_rows = [prior_buffer[survey, :, at, :] for at in range(layers)]
        for at in range(layers):
            flat_refs[survey][:, at * layer_cells : (at + 1) * layer_cells] = layer_rows[at]
        edge_ref[survey] = jnp.where(upward, layer_rows[0], layer_rows[-1])
    ids_copy.wait()
    lane = lax.broadcasted_iota(jnp.int32, (model_count, LANES), 1)
    for survey in range(surveys):
        ids = jnp.broadcast_to(ids_buffer[survey : survey + 1], (model_count, stations))
        counts = jnp.zeros((model_count, LANES), F32)
        for label in range(NSURV):
            here = jnp.sum((ids == label).astype(F32), axis=1, keepdims=True)
            counts = jnp.where(lane == NSURV + label, here, counts)
        count_ref[survey] = counts
    for survey in range(surveys):
        rows = split_rows(flat_refs[survey][...])

        def step_fn(at, carry):
            step = survey * per_survey + at
            copy(step).wait()

            @pl.when(step + slots - 1 < total)
            def _():
                copy(step + slots - 1).start()

            place = pl.ds(pl.multiple_of(at * block, block), block)
            values = buffers[step % slots]
            high = values.astype(BF16)
            low = (values - high.astype(F32)).astype(BF16)
            split_ref[0, survey, place, :] = high
            split_ref[1, survey, place, :] = low
            turned = values.T
            high_t = turned.astype(BF16)
            turned_ref[0, survey, :, place] = high_t
            turned_ref[1, survey, :, place] = (turned - high_t.astype(F32)).astype(BF16)
            part_ref[survey, :, place] = fold_rows(dot(rows, high, 1) + dot(rows, low, 1))
            return carry

        lax.fori_loop(0, per_survey, step_fn, 0)


def prepare(sens, prior, ids):
    surveys, stations, cells = sens.shape
    _, model_count, _, layer_cells = prior.shape
    block = min(stations, LANES)
    slots = 5
    outs = pl.pallas_call(
        functools.partial(prepare_kernel, block),
        out_shape=[
            pltpu.VMEM((2, surveys, stations, cells), BF16),
            pltpu.VMEM((2, surveys, cells, stations), BF16),
            jax.ShapeDtypeStruct((surveys, model_count, stations), F32),
            jax.ShapeDtypeStruct((surveys, model_count, LANES), F32),
            jax.ShapeDtypeStruct((surveys, model_count, layer_cells), F32),
        ]
        + [jax.ShapeDtypeStruct((model_count, cells), F32)] * surveys,
        in_specs=[IN_HBM] * 3,
        out_specs=[IN_VMEM] * (5 + surveys),
        scratch_shapes=[
            pltpu.VMEM((slots, block, cells), F32),
            pltpu.VMEM(prior.shape, F32),
            pltpu.VMEM(ids.shape, jnp.int32),
            pltpu.SemaphoreType.DMA((slots,)),
            pltpu.SemaphoreType.DMA((2,)),
        ],
        compiler_params=pltpu.CompilerParams(vmem_limit_bytes=12 * MIB),
        name="prepare",
    )(*[pltpu.with_memory_space_constraint(x, pltpu.HBM) for x in (sens, prior, ids)])
    return *outs[:5], list(outs[5:])


def stepped(models, prior, own, other):
    return models - step_size * ((own + other) + prior_weight * (models - prior))


def forward_kernel(survey, *refs):
    models_ref, prior_ref, own_ref, other_ref, turned_ref = refs[:5]
    models = stepped(models_ref[...], prior_ref[...], own_ref[...], other_ref[...])
    rows = split_rows(models)
    part = fold_rows(dot(rows, turned_ref[0, survey]) + dot(rows, turned_ref[1, survey]))
    refs = refs[5:]
    if survey + 1 < turned_ref.shape[1]:
        next_ref, part_ref = refs
        next_ref[...] = models
        part_ref[...] = part
        return
    earlier_models = refs[:survey]
    earlier_parts = refs[survey : 2 * survey]
    next_ref, edge_ref, part_ref = refs[2 * survey :]
    next_ref[...] = models
    part_ref[survey] = part
    for at in range(survey):
        part_ref[at] = earlier_parts[at][...]
    cells = models.shape[1]
    layer_cells = edge_ref.shape[2]
    upward = lax.axis_index("dp") == 0
    for at, ref in enumerate((*earlier_models, next_ref)):
        edge_ref[at] = jnp.where(
            upward, ref[:, :layer_cells], ref[:, cells - layer_cells :]
        )


def forward(models, prior, owns, others, turned, layer_cells):
    surveys = len(models)
    model_count, _ = models[0].shape
    stations = turned.shape[3]
    moved = []
    parts = []
    for survey in range(surveys):
        out_shape = [jax.ShapeDtypeStruct(models[survey].shape, F32)]
        operands = [models[survey], prior[survey], owns[survey], others[survey], resident(turned)]
        if survey + 1 < surveys:
            out_shape += [jax.ShapeDtypeStruct((model_count, stations), F32)]
        else:
            operands += moved + parts
            out_shape += [
                jax.ShapeDtypeStruct((surveys, model_count, layer_cells), F32),
                jax.ShapeDtypeStruct((surveys, model_count, stations), F32),
            ]
        outs = pl.pallas_call(
            functools.partial(forward_kernel, survey),
            out_shape=out_shape,
            in_specs=[IN_VMEM] * len(operands),
            out_specs=[IN_VMEM] * len(out_shape),
            compiler_params=pltpu.CompilerParams(vmem_limit_bytes=4 * MIB),
            cost_estimate=product_cost(turned),
            name="forward",
        )(*operands)
        moved.append(outs[0])
        parts.append(outs[1])
    return moved, outs[1], outs[2]


def product_cost(split):
    cells = split.shape[2] * split.shape[3]
    return pl.CostEstimate(flops=512 * cells, bytes_accessed=4 * cells, transcendentals=0)


def cross_terms(field, above, keep_x, keep_y, keep_z, depth_only):
    cells = field[0].shape[1]
    first = []
    second = []
    for grads, here, deeper in zip((first, second), field, above):
        grads.append((pltpu.roll(here, cells - 1, 1) - here) * keep_x)
        grads.append((pltpu.roll(here, cells - NX, 1) - here) * keep_y)
        change = deeper - here
        grads.append(change if keep_z is None else change * keep_z)
    cross_x = first[1] * second[2] - first[2] * second[1]
    cross_y = first[2] * second[0] - first[0] * second[2]
    cross_z = first[0] * second[1] - first[1] * second[0]
    scaling = (2.0 * couple_weight) / (
        1.0 + cross_x * cross_x + cross_y * cross_y + cross_z * cross_z
    )
    depth = [
        scaling * (second[0] * cross_y - second[1] * cross_x),
        scaling * (cross_x * first[1] - cross_y * first[0]),
    ]
    if keep_z is not None:
        depth = [value * keep_z for value in depth]
    if depth_only:
        return depth, None
    grad_x = [
        scaling * (second[1] * cross_z - second[2] * cross_y) * keep_x,
        scaling * (cross_y * first[2] - cross_z * first[1]) * keep_x,
    ]
    grad_y = [
        scaling * (second[2] * cross_x - second[0] * cross_z) * keep_y,
        scaling * (cross_z * first[0] - cross_x * first[2]) * keep_y,
    ]
    level = [
        (pltpu.roll(along_x, 1, 1) - along_x) + (pltpu.roll(along_y, NX, 1) - along_y)
        for along_x, along_y in zip(grad_x, grad_y)
    ]
    return depth, level


def couple_kernel(layer_cells, *refs):
    models_refs, edge_ref, out_refs = refs[:2], refs[2], refs[3:]
    model_count, cells = models_refs[0].shape
    layers = cells // layer_cells
    middle = layers // 2
    place = lax.broadcasted_iota(jnp.int32, (model_count, layer_cells), 1)
    keep_x = (place % NX < NX - 1).astype(F32)
    keep_y = (place < layer_cells - NX).astype(F32)
    side = lax.axis_index("dp")
    index = lax.axis_index("cell")

    def layer(at):
        if 0 <= at < layers:
            return [
                ref[:, at * layer_cells : (at + 1) * layer_cells] for ref in models_refs
            ]
        return [edge_ref[survey] for survey in range(2)]

    def write(start, stop):
        sums = {}

        def add(at, values):
            if 0 <= at < layers:
                sums[at] = values if at not in sums else [a + b for a, b in zip(sums[at], values)]

        for at in range(start, stop):
            keep_z = None
            if at < 0:
                keep_z = jnp.where(index > 0, 1.0, 0.0).astype(F32)
            elif at == layers - 1:
                keep_z = jnp.where(index < lax.axis_size("cell") - 1, 1.0, 0.0).astype(F32)
            depth, level = cross_terms(layer(at), layer(at + 1), keep_x, keep_y, keep_z, at < 0)
            if level is not None:
                add(at, [value - below for value, below in zip(level, depth)])
            add(at + 1, depth)
        for at in range(layers):
            for survey in range(2):
                spot = slice(at * layer_cells, (at + 1) * layer_cells)
                if at in sums:
                    out_refs[survey][:, spot] = sums[at][survey]
                else:
                    out_refs[survey][:, spot] = jnp.zeros((model_count, layer_cells), F32)

    @pl.when(side == 0)
    def _():
        write(middle, layers)

    @pl.when(side != 0)
    def _():
        write(-1, middle)


def couple_share(models, edge, layer_cells):
    return pl.pallas_call(
        functools.partial(couple_kernel, layer_cells),
        out_shape=[jax.ShapeDtypeStruct(x.shape, F32) for x in models],
        in_specs=[IN_VMEM] * 3,
        out_specs=[IN_VMEM] * 2,
        compiler_params=pltpu.CompilerParams(vmem_limit_bytes=4 * MIB),
        name="couple",
    )(*models, edge)


def residual_kernel(
    here_ref, there_ref, observed_ref, noise_ref, perturb_ref, ids_ref, count_ref, resid_ref, sums_ref
):
    surveys, model_count, stations = here_ref.shape
    lane = lax.broadcasted_iota(jnp.int32, (model_count, LANES), 1)
    for survey in range(surveys):
        noise = noise_ref[survey : survey + 1]
        targets = observed_ref[survey : survey + 1] + noise * perturb_ref[survey]
        resid = ((here_ref[survey] + there_ref[survey]) - targets) / noise
        resid_ref[survey] = resid
        squares = resid * resid
        ids = jnp.broadcast_to(ids_ref[survey : survey + 1], (model_count, stations))
        sums = count_ref[survey]
        for label in range(NSURV):
            here = jnp.sum(jnp.where(ids == label, squares, 0.0), axis=1, keepdims=True)
            sums = jnp.where(lane == label, here, sums)
        sums_ref[survey] = sums


def residual(here, there, observed, noise, perturb, ids, counts):
    return pl.pallas_call(
        residual_kernel,
        out_shape=[
            jax.ShapeDtypeStruct(here.shape, F32),
            jax.ShapeDtypeStruct(counts.shape, F32),
        ],
        in_specs=[IN_VMEM] * 7,
        out_specs=[IN_VMEM] * 2,
        compiler_params=pltpu.CompilerParams(vmem_limit_bytes=4 * MIB),
        name="residual",
    )(here, there, observed, noise, perturb, ids, counts)


def backward_kernel(
    survey, resid_ref, own_ref, other_ref, noise_ref, ids_ref, couple_ref, split_ref, out_ref
):
    _, model_count, stations = resid_ref.shape
    sums = own_ref[survey] + other_ref[survey]
    counts = pltpu.roll(sums, LANES - NSURV, 1)
    spread = (sums + 1.0) / (counts + 1.0)
    ids = jnp.broadcast_to(ids_ref[survey : survey + 1], (model_count, stations))
    spread_rows = jnp.zeros((model_count, stations), F32)
    for label in range(NSURV):
        spread_rows = jnp.where(ids == label, spread[:, label : label + 1], spread_rows)
    resid = resid_ref[survey]
    factor = (nu_value + 1.0) * resid / (
        noise_ref[survey : survey + 1] * (nu_value * spread_rows + resid * resid)
    )
    rows = split_rows(factor)
    out_ref[...] = couple_ref[...] + fold_rows(
        dot(rows, split_ref[0, survey]) + dot(rows, split_ref[1, survey])
    )


def backward(survey, resid, own, other, noise, ids, couple, split):
    return pl.pallas_call(
        functools.partial(backward_kernel, survey),
        out_shape=jax.ShapeDtypeStruct(couple.shape, F32),
        in_specs=[IN_VMEM] * 7,
        out_specs=IN_VMEM,
        compiler_params=pltpu.CompilerParams(vmem_limit_bytes=4 * MIB),
        cost_estimate=product_cost(split),
        name="backward",
    )(resid, own, other, noise, ids, couple, resident(split))


def step_kernel(models_ref, prior_ref, own_ref, other_ref, next_ref):
    next_ref[...] = stepped(models_ref[...], prior_ref[...], own_ref[...], other_ref[...])


def finish_kernel(*refs):
    out_ref = refs[-1]
    surveys, _, layers, layer_cells = out_ref.shape
    for survey in range(surveys):
        ready = survey + 1 < surveys
        models = refs[survey][...] if ready else stepped(*[ref[...] for ref in refs[survey:-1]])
        for at in range(layers):
            out_ref[survey, :, at, :] = models[:, at * layer_cells : (at + 1) * layer_cells]


def finish(models, prior, owns, others, shape):
    operands = []
    for survey in range(shape[0]):
        mine = [models[survey], prior[survey], owns[survey], others[survey]]
        if survey + 1 < shape[0]:
            mine = [
                pl.pallas_call(
                    step_kernel,
                    out_shape=jax.ShapeDtypeStruct(models[survey].shape, F32),
                    in_specs=[IN_VMEM] * 4,
                    out_specs=IN_VMEM,
                    compiler_params=pltpu.CompilerParams(vmem_limit_bytes=4 * MIB),
                    name="step",
                )(*mine)
            ]
        operands += mine
    return pl.pallas_call(
        finish_kernel,
        out_shape=jax.ShapeDtypeStruct(shape, F32),
        in_specs=[IN_VMEM] * len(operands),
        out_specs=IN_VMEM,
        compiler_params=pltpu.CompilerParams(vmem_limit_bytes=4 * MIB),
        name="finish",
    )(*operands)


def from_pair(values):
    return lax.ppermute(values, "dp", [(0, 1), (1, 0)])


def exchange_edges(edge):
    devices = lax.axis_size("cell")
    pairs = [(2 * i, 2 * i - 2) for i in range(1, devices)]
    pairs += [(2 * i + 1, 2 * i + 3) for i in range(devices - 1)]
    return lax.ppermute(edge, ("cell", "dp"), pairs)


def fetch(values, by, devices):
    return lax.ppermute(values, "cell", [(i, i ^ by) for i in range(devices)])


def cell_pair(values):
    devices = lax.axis_size("cell")
    stride = devices
    while stride > 2:
        base = 4 if stride >= 8 else 2
        stride //= base
        total = values
        for count in range(1, base):
            total = total + fetch(values, count * stride, devices)
        values = total
    return values, fetch(values, 1, devices)


def body(sens, observed, noise, ids, data_perturb, prior):
    surveys, _, _, layer_cells = prior.shape
    split, turned, part, counts, edge, flat = prepare(sens, prior, ids)
    models = flat
    for iteration in range(ITERS):
        if iteration:
            models, edge, part = forward(models, flat, owns, others, turned, layer_cells)
        edge = exchange_edges(edge)
        here, there = cell_pair(part)
        couple = couple_share(models, edge, layer_cells)
        resid, own_sums = residual(here, there, observed, noise, data_perturb, ids, counts)
        other_sums = from_pair(own_sums)
        owns = []
        others = []
        for survey in range(surveys):
            own = backward(
                survey, resid, own_sums, other_sums, noise, ids, couple[survey], split
            )
            owns.append(own)
            others.append(from_pair(own))
    return finish(models, flat, owns, others, prior.shape)


def solution(mesh):
    return jax.shard_map(
        body,
        mesh=mesh,
        in_specs=(
            P(None, ("slab", "dp"), "cell"),
            P(None, ("slab", "dp")),
            P(None, ("slab", "dp")),
            P(None, ("slab", "dp")),
            P(None, None, ("slab", "dp")),
            P(None, "slab", "cell", None),
        ),
        out_specs=P(None, "slab", "cell", None),
        check_vma=False,
    )
```

```python
import functools

import jax
import jax.numpy as jnp
from jax import lax
from jax.experimental import pallas as pl
from jax.experimental.pallas import tpu as pltpu
from jax.sharding import PartitionSpec as P

NX = 32
NSURV = 8
ITERS = 4

nu_value = 4.0
step_size = 0.5
couple_weight = 0.02
prior_weight = 0.1

LANES = 128
MIB = 2**20
BF16 = jnp.bfloat16
F32 = jnp.float32
IN_VMEM = pl.BlockSpec(memory_space=pltpu.VMEM)
IN_HBM = pl.BlockSpec(memory_space=pltpu.HBM)


def dot(left, right, along=0):
    return lax.dot_general(
        left, right, (((1,), (along,)), ((), ())), preferred_element_type=F32
    )


def resident(values):
    return pltpu.with_memory_space_constraint(values, pltpu.VMEM)


def split_rows(values):
    high = values.astype(BF16).astype(F32)
    return jnp.concatenate([high, values - high], axis=0).astype(BF16)


def fold_rows(values):
    half = values.shape[0] // 2
    return values[:half] + values[half:]


def prepare_kernel(
    block,
    sens_ref,
    prior_ref,
    ids_ref,
    split_ref,
    turned_ref,
    part_ref,
    count_ref,
    edge_ref,
    *rest,
):
    surveys, stations, _ = sens_ref.shape
    _, model_count, layers, layer_cells = prior_ref.shape
    flat_refs = rest[:surveys]
    buffers, prior_buffer, ids_buffer, semaphores, small_semaphores = rest[surveys:]
    per_survey = stations // block
    total = surveys * per_survey
    slots = buffers.shape[0]

    def copy(step):
        start = pl.multiple_of((step % per_survey) * block, block)
        slot = step % slots
        return pltpu.make_async_copy(
            sens_ref.at[step // per_survey, pl.ds(start, block), :],
            buffers.at[slot],
            semaphores.at[slot],
        )

    prior_copy = pltpu.make_async_copy(prior_ref, prior_buffer, small_semaphores.at[0])
    ids_copy = pltpu.make_async_copy(ids_ref, ids_buffer, small_semaphores.at[1])
    ahead = min(slots - 1, total)
    prior_copy.start()
    ids_copy.start()
    for step in range(min(2, ahead)):
        copy(step).start()
    prior_copy.wait()
    for step in range(min(2, ahead), ahead):
        copy(step).start()
    downward = lax.axis_index("dp") == 0
    for survey in range(surveys):
        layer_rows = [prior_buffer[survey, :, at, :] for at in range(layers)]
        for at in range(layers):
            flat_refs[survey][:, at * layer_cells : (at + 1) * layer_cells] = layer_rows[at]
        edge_ref[survey] = jnp.where(downward, layer_rows[-1], layer_rows[0])
    ids_copy.wait()
    lane = lax.broadcasted_iota(jnp.int32, (model_count, LANES), 1)
    for survey in range(surveys):
        ids = jnp.broadcast_to(ids_buffer[survey : survey + 1], (model_count, stations))
        counts = jnp.zeros((model_count, LANES), F32)
        for label in range(NSURV):
            here = jnp.sum((ids == label).astype(F32), axis=1, keepdims=True)
            counts = jnp.where(lane == NSURV + label, here, counts)
        count_ref[survey] = counts
    for survey in range(surveys):
        rows = split_rows(flat_refs[survey][...])

        def step_fn(at, carry):
            step = survey * per_survey + at
            copy(step).wait()

            @pl.when(step + slots - 1 < total)
            def _():
                copy(step + slots - 1).start()

            place = pl.ds(pl.multiple_of(at * block, block), block)
            values = buffers[step % slots]
            high = values.astype(BF16)
            low = (values - high.astype(F32)).astype(BF16)
            split_ref[0, survey, place, :] = high
            split_ref[1, survey, place, :] = low
            turned = values.T
            high_t = turned.astype(BF16)
            turned_ref[0, survey, :, place] = high_t
            turned_ref[1, survey, :, place] = (turned - high_t.astype(F32)).astype(BF16)
            part_ref[survey, :, place] = fold_rows(dot(rows, high, 1) + dot(rows, low, 1))
            return carry

        lax.fori_loop(0, per_survey, step_fn, 0)


def prepare(sens, prior, ids):
    surveys, stations, cells = sens.shape
    _, model_count, _, layer_cells = prior.shape
    block = min(stations, LANES)
    slots = 5
    outs = pl.pallas_call(
        functools.partial(prepare_kernel, block),
        out_shape=[
            pltpu.VMEM((2, surveys, stations, cells), BF16),
            pltpu.VMEM((2, surveys, cells, stations), BF16),
            jax.ShapeDtypeStruct((surveys, model_count, stations), F32),
            jax.ShapeDtypeStruct((surveys, model_count, LANES), F32),
            jax.ShapeDtypeStruct((surveys, model_count, layer_cells), F32),
        ]
        + [jax.ShapeDtypeStruct((model_count, cells), F32)] * surveys,
        in_specs=[IN_HBM] * 3,
        out_specs=[IN_VMEM] * (5 + surveys),
        scratch_shapes=[
            pltpu.VMEM((slots, block, cells), F32),
            pltpu.VMEM(prior.shape, F32),
            pltpu.VMEM(ids.shape, jnp.int32),
            pltpu.SemaphoreType.DMA((slots,)),
            pltpu.SemaphoreType.DMA((2,)),
        ],
        compiler_params=pltpu.CompilerParams(vmem_limit_bytes=12 * MIB),
        name="prepare",
    )(*[pltpu.with_memory_space_constraint(x, pltpu.HBM) for x in (sens, prior, ids)])
    return *outs[:5], list(outs[5:])


def stepped(models, prior, own, other):
    return models - step_size * ((own + other) + prior_weight * (models - prior))


def forward_kernel(survey, *refs):
    models_ref, prior_ref, own_ref, other_ref, turned_ref = refs[:5]
    models = stepped(models_ref[...], prior_ref[...], own_ref[...], other_ref[...])
    rows = split_rows(models)
    part = fold_rows(dot(rows, turned_ref[0, survey]) + dot(rows, turned_ref[1, survey]))
    refs = refs[5:]
    if survey + 1 < turned_ref.shape[1]:
        next_ref, part_ref = refs
        next_ref[...] = models
        part_ref[...] = part
        return
    earlier_models = refs[:survey]
    earlier_parts = refs[survey : 2 * survey]
    next_ref, edge_ref, part_ref = refs[2 * survey :]
    next_ref[...] = models
    part_ref[survey] = part
    for at in range(survey):
        part_ref[at] = earlier_parts[at][...]
    cells = models.shape[1]
    layer_cells = edge_ref.shape[2]
    downward = lax.axis_index("dp") == 0
    for at, ref in enumerate((*earlier_models, next_ref)):
        edge_ref[at] = jnp.where(
            downward, ref[:, cells - layer_cells :], ref[:, :layer_cells]
        )


def forward(models, prior, owns, others, turned, layer_cells):
    surveys = len(models)
    model_count, _ = models[0].shape
    stations = turned.shape[3]
    moved = []
    parts = []
    for survey in range(surveys):
        out_shape = [jax.ShapeDtypeStruct(models[survey].shape, F32)]
        operands = [models[survey], prior[survey], owns[survey], others[survey], resident(turned)]
        if survey + 1 < surveys:
            out_shape += [jax.ShapeDtypeStruct((model_count, stations), F32)]
        else:
            operands += moved + parts
            out_shape += [
                jax.ShapeDtypeStruct((surveys, model_count, layer_cells), F32),
                jax.ShapeDtypeStruct((surveys, model_count, stations), F32),
            ]
        outs = pl.pallas_call(
            functools.partial(forward_kernel, survey),
            out_shape=out_shape,
            in_specs=[IN_VMEM] * len(operands),
            out_specs=[IN_VMEM] * len(out_shape),
            compiler_params=pltpu.CompilerParams(vmem_limit_bytes=4 * MIB),
            cost_estimate=product_cost(turned),
            name="forward",
        )(*operands)
        moved.append(outs[0])
        parts.append(outs[1])
    return moved, outs[1], outs[2]


def product_cost(split):
    cells = split.shape[2] * split.shape[3]
    return pl.CostEstimate(flops=512 * cells, bytes_accessed=4 * cells, transcendentals=0)


def cross_terms(field, above, keep_x, keep_y, keep_z, depth_only):
    cells = field[0].shape[1]
    first = []
    second = []
    for grads, here, deeper in zip((first, second), field, above):
        grads.append((pltpu.roll(here, cells - 1, 1) - here) * keep_x)
        grads.append((pltpu.roll(here, cells - NX, 1) - here) * keep_y)
        change = deeper - here
        grads.append(change if keep_z is None else change * keep_z)
    cross_x = first[1] * second[2] - first[2] * second[1]
    cross_y = first[2] * second[0] - first[0] * second[2]
    cross_z = first[0] * second[1] - first[1] * second[0]
    scaling = (2.0 * couple_weight) / (
        1.0 + cross_x * cross_x + cross_y * cross_y + cross_z * cross_z
    )
    depth = [
        scaling * (second[0] * cross_y - second[1] * cross_x),
        scaling * (cross_x * first[1] - cross_y * first[0]),
    ]
    if keep_z is not None:
        depth = [value * keep_z for value in depth]
    if depth_only:
        return depth, None
    grad_x = [
        scaling * (second[1] * cross_z - second[2] * cross_y) * keep_x,
        scaling * (cross_y * first[2] - cross_z * first[1]) * keep_x,
    ]
    grad_y = [
        scaling * (second[2] * cross_x - second[0] * cross_z) * keep_y,
        scaling * (cross_z * first[0] - cross_x * first[2]) * keep_y,
    ]
    level = [
        (pltpu.roll(along_x, 1, 1) - along_x) + (pltpu.roll(along_y, NX, 1) - along_y)
        for along_x, along_y in zip(grad_x, grad_y)
    ]
    return depth, level


def couple_kernel(layer_cells, *refs):
    models_refs, edge_ref, out_refs = refs[:2], refs[2], refs[3:]
    model_count, cells = models_refs[0].shape
    layers = cells // layer_cells
    middle = layers // 2
    place = lax.broadcasted_iota(jnp.int32, (model_count, layer_cells), 1)
    keep_x = (place % NX < NX - 1).astype(F32)
    keep_y = (place < layer_cells - NX).astype(F32)
    side = lax.axis_index("dp")
    index = lax.axis_index("cell")

    def layer(at):
        if 0 <= at < layers:
            return [
                ref[:, at * layer_cells : (at + 1) * layer_cells] for ref in models_refs
            ]
        return [edge_ref[survey] for survey in range(2)]

    def write(start, stop):
        sums = {}

        def add(at, values):
            if 0 <= at < layers:
                sums[at] = values if at not in sums else [a + b for a, b in zip(sums[at], values)]

        for at in range(start, stop):
            keep_z = None
            if at < 0:
                keep_z = jnp.where(index > 0, 1.0, 0.0).astype(F32)
            elif at == layers - 1:
                keep_z = jnp.where(index < lax.axis_size("cell") - 1, 1.0, 0.0).astype(F32)
            depth, level = cross_terms(layer(at), layer(at + 1), keep_x, keep_y, keep_z, at < 0)
            if level is not None:
                add(at, [value - below for value, below in zip(level, depth)])
            add(at + 1, depth)
        for at in range(layers):
            for survey in range(2):
                spot = slice(at * layer_cells, (at + 1) * layer_cells)
                if at in sums:
                    out_refs[survey][:, spot] = sums[at][survey]
                else:
                    out_refs[survey][:, spot] = jnp.zeros((model_count, layer_cells), F32)

    @pl.when(side == 0)
    def _():
        write(middle, layers)

    @pl.when(side != 0)
    def _():
        write(-1, middle)


def couple_share(models, edge, layer_cells):
    return pl.pallas_call(
        functools.partial(couple_kernel, layer_cells),
        out_shape=[jax.ShapeDtypeStruct(x.shape, F32) for x in models],
        in_specs=[IN_VMEM] * 3,
        out_specs=[IN_VMEM] * 2,
        compiler_params=pltpu.CompilerParams(vmem_limit_bytes=4 * MIB),
        name="couple",
    )(*models, edge)


def residual_kernel(
    here_ref, there_ref, observed_ref, noise_ref, perturb_ref, ids_ref, count_ref, resid_ref, sums_ref
):
    surveys, model_count, stations = here_ref.shape
    lane = lax.broadcasted_iota(jnp.int32, (model_count, LANES), 1)
    for survey in range(surveys):
        noise = noise_ref[survey : survey + 1]
        targets = observed_ref[survey : survey + 1] + noise * perturb_ref[survey]
        resid = ((here_ref[survey] + there_ref[survey]) - targets) / noise
        resid_ref[survey] = resid
        squares = resid * resid
        ids = jnp.broadcast_to(ids_ref[survey : survey + 1], (model_count, stations))
        sums = count_ref[survey]
        for label in range(NSURV):
            here = jnp.sum(jnp.where(ids == label, squares, 0.0), axis=1, keepdims=True)
            sums = jnp.where(lane == label, here, sums)
        sums_ref[survey] = sums


def residual(here, there, observed, noise, perturb, ids, counts):
    return pl.pallas_call(
        residual_kernel,
        out_shape=[
            jax.ShapeDtypeStruct(here.shape, F32),
            jax.ShapeDtypeStruct(counts.shape, F32),
        ],
        in_specs=[IN_VMEM] * 7,
        out_specs=[IN_VMEM] * 2,
        compiler_params=pltpu.CompilerParams(vmem_limit_bytes=4 * MIB),
        name="residual",
    )(here, there, observed, noise, perturb, ids, counts)


def backward_kernel(
    survey, resid_ref, own_ref, other_ref, noise_ref, ids_ref, couple_ref, split_ref, out_ref
):
    _, model_count, stations = resid_ref.shape
    sums = own_ref[survey] + other_ref[survey]
    counts = pltpu.roll(sums, LANES - NSURV, 1)
    spread = (sums + 1.0) / (counts + 1.0)
    ids = jnp.broadcast_to(ids_ref[survey : survey + 1], (model_count, stations))
    spread_rows = jnp.zeros((model_count, stations), F32)
    for label in range(NSURV):
        spread_rows = jnp.where(ids == label, spread[:, label : label + 1], spread_rows)
    resid = resid_ref[survey]
    factor = (nu_value + 1.0) * resid / (
        noise_ref[survey : survey + 1] * (nu_value * spread_rows + resid * resid)
    )
    rows = split_rows(factor)
    out_ref[...] = couple_ref[...] + fold_rows(
        dot(rows, split_ref[0, survey]) + dot(rows, split_ref[1, survey])
    )


def backward(survey, resid, own, other, noise, ids, couple, split):
    return pl.pallas_call(
        functools.partial(backward_kernel, survey),
        out_shape=jax.ShapeDtypeStruct(couple.shape, F32),
        in_specs=[IN_VMEM] * 7,
        out_specs=IN_VMEM,
        compiler_params=pltpu.CompilerParams(vmem_limit_bytes=4 * MIB),
        cost_estimate=product_cost(split),
        name="backward",
    )(resid, own, other, noise, ids, couple, resident(split))


def step_kernel(models_ref, prior_ref, own_ref, other_ref, next_ref):
    next_ref[...] = stepped(models_ref[...], prior_ref[...], own_ref[...], other_ref[...])


def finish_kernel(*refs):
    out_ref = refs[-1]
    surveys, _, layers, layer_cells = out_ref.shape
    for survey in range(surveys):
        ready = survey + 1 < surveys
        models = refs[survey][...] if ready else stepped(*[ref[...] for ref in refs[survey:-1]])
        for at in range(layers):
            out_ref[survey, :, at, :] = models[:, at * layer_cells : (at + 1) * layer_cells]


def finish(models, prior, owns, others, shape):
    operands = []
    for survey in range(shape[0]):
        mine = [models[survey], prior[survey], owns[survey], others[survey]]
        if survey + 1 < shape[0]:
            mine = [
                pl.pallas_call(
                    step_kernel,
                    out_shape=jax.ShapeDtypeStruct(models[survey].shape, F32),
                    in_specs=[IN_VMEM] * 4,
                    out_specs=IN_VMEM,
                    compiler_params=pltpu.CompilerParams(vmem_limit_bytes=4 * MIB),
                    name="step",
                )(*mine)
            ]
        operands += mine
    return pl.pallas_call(
        finish_kernel,
        out_shape=jax.ShapeDtypeStruct(shape, F32),
        in_specs=[IN_VMEM] * len(operands),
        out_specs=IN_VMEM,
        compiler_params=pltpu.CompilerParams(vmem_limit_bytes=4 * MIB),
        name="finish",
    )(*operands)


def from_pair(values):
    return lax.ppermute(values, "dp", [(0, 1), (1, 0)])


def exchange_edges(edge):
    devices = lax.axis_size("cell")
    pairs = [(2 * i, 2 * i + 3) for i in range(devices - 1)]
    pairs += [(2 * i + 3, 2 * i) for i in range(devices - 1)]
    return lax.ppermute(edge, ("cell", "dp"), pairs)


def fetch(values, by, devices):
    return lax.ppermute(values, "cell", [(i, i ^ by) for i in range(devices)])


def cell_pair(values):
    devices = lax.axis_size("cell")
    stride = devices
    while stride > 2:
        base = 4 if stride >= 8 else 2
        stride //= base
        total = values
        for count in range(1, base):
            total = total + fetch(values, count * stride, devices)
        values = total
    return values, fetch(values, 1, devices)


def body(sens, observed, noise, ids, data_perturb, prior):
    surveys, _, _, layer_cells = prior.shape
    split, turned, part, counts, edge, flat = prepare(sens, prior, ids)
    models = flat
    for iteration in range(ITERS):
        if iteration:
            models, edge, part = forward(models, flat, owns, others, turned, layer_cells)
        edge = exchange_edges(edge)
        here, there = cell_pair(part)
        couple = couple_share(models, edge, layer_cells)
        resid, own_sums = residual(here, there, observed, noise, data_perturb, ids, counts)
        other_sums = from_pair(own_sums)
        owns = []
        others = []
        for survey in range(surveys):
            own = backward(
                survey, resid, own_sums, other_sums, noise, ids, couple[survey], split
            )
            owns.append(own)
            others.append(from_pair(own))
    return finish(models, flat, owns, others, prior.shape)


def solution(mesh):
    return jax.shard_map(
        body,
        mesh=mesh,
        in_specs=(
            P(None, ("slab", "dp"), "cell"),
            P(None, ("slab", "dp")),
            P(None, ("slab", "dp")),
            P(None, ("slab", "dp")),
            P(None, None, ("slab", "dp")),
            P(None, "slab", "cell", None),
        ),
        out_specs=P(None, "slab", "cell", None),
        check_vma=False,
    )
```

```python
import functools

import jax
import jax.numpy as jnp
from jax import lax
from jax.experimental import pallas as pl
from jax.experimental.pallas import tpu as pltpu
from jax.sharding import PartitionSpec as P

NX = 32
NSURV = 8
ITERS = 4

nu_value = 4.0
step_size = 0.5
couple_weight = 0.02
prior_weight = 0.1

LANES = 128
MIB = 2**20
BF16 = jnp.bfloat16
F32 = jnp.float32
IN_VMEM = pl.BlockSpec(memory_space=pltpu.VMEM)
IN_HBM = pl.BlockSpec(memory_space=pltpu.HBM)


def dot(left, right, along=0):
    return lax.dot_general(
        left, right, (((1,), (along,)), ((), ())), preferred_element_type=F32
    )


def resident(values):
    return pltpu.with_memory_space_constraint(values, pltpu.VMEM)


def split_rows(values):
    high = values.astype(BF16).astype(F32)
    return jnp.concatenate([high, values - high], axis=0).astype(BF16)


def fold_rows(values):
    half = values.shape[0] // 2
    return values[:half] + values[half:]


def prepare_kernel(
    block,
    sens_ref,
    prior_ref,
    ids_ref,
    split_ref,
    turned_ref,
    part_ref,
    count_ref,
    edge_ref,
    *rest,
):
    surveys, stations, _ = sens_ref.shape
    _, model_count, layers, layer_cells = prior_ref.shape
    flat_refs = rest[:surveys]
    buffers, prior_buffer, ids_buffer, semaphores, small_semaphores = rest[surveys:]
    per_survey = stations // block
    total = surveys * per_survey
    slots = buffers.shape[0]

    def copy(step):
        start = pl.multiple_of((step % per_survey) * block, block)
        slot = step % slots
        return pltpu.make_async_copy(
            sens_ref.at[step // per_survey, pl.ds(start, block), :],
            buffers.at[slot],
            semaphores.at[slot],
        )

    prior_copy = pltpu.make_async_copy(prior_ref, prior_buffer, small_semaphores.at[0])
    ids_copy = pltpu.make_async_copy(ids_ref, ids_buffer, small_semaphores.at[1])
    ahead = min(slots - 1, total)
    prior_copy.start()
    ids_copy.start()
    for step in range(min(2, ahead)):
        copy(step).start()
    prior_copy.wait()
    for step in range(min(2, ahead), ahead):
        copy(step).start()
    downward = lax.axis_index("dp") == 0
    for survey in range(surveys):
        layer_rows = [prior_buffer[survey, :, at, :] for at in range(layers)]
        for at in range(layers):
            flat_refs[survey][:, at * layer_cells : (at + 1) * layer_cells] = layer_rows[at]
        edge_ref[survey] = jnp.where(downward, layer_rows[-1], layer_rows[0])
    ids_copy.wait()
    lane = lax.broadcasted_iota(jnp.int32, (model_count, LANES), 1)
    for survey in range(surveys):
        ids = jnp.broadcast_to(ids_buffer[survey : survey + 1], (model_count, stations))
        counts = jnp.zeros((model_count, LANES), F32)
        for label in range(NSURV):
            here = jnp.sum((ids == label).astype(F32), axis=1, keepdims=True)
            counts = jnp.where(lane == NSURV + label, here, counts)
        count_ref[survey] = counts
    for survey in range(surveys):
        rows = split_rows(flat_refs[survey][...])

        def step_fn(at, carry):
            step = survey * per_survey + at
            copy(step).wait()

            @pl.when(step + slots - 1 < total)
            def _():
                copy(step + slots - 1).start()

            place = pl.ds(pl.multiple_of(at * block, block), block)
            values = buffers[step % slots]
            high = values.astype(BF16)
            low = (values - high.astype(F32)).astype(BF16)
            split_ref[0, survey, place, :] = high
            split_ref[1, survey, place, :] = low
            turned = values.T
            high_t = turned.astype(BF16)
            turned_ref[0, survey, :, place] = high_t
            turned_ref[1, survey, :, place] = (turned - high_t.astype(F32)).astype(BF16)
            part_ref[survey, :, place] = fold_rows(dot(rows, high, 1) + dot(rows, low, 1))
            return carry

        lax.fori_loop(0, per_survey, step_fn, 0)


def prepare(sens, prior, ids):
    surveys, stations, cells = sens.shape
    _, model_count, _, layer_cells = prior.shape
    block = min(stations, LANES)
    slots = 5
    outs = pl.pallas_call(
        functools.partial(prepare_kernel, block),
        out_shape=[
            pltpu.VMEM((2, surveys, stations, cells), BF16),
            pltpu.VMEM((2, surveys, cells, stations), BF16),
            jax.ShapeDtypeStruct((surveys, model_count, stations), F32),
            jax.ShapeDtypeStruct((surveys, model_count, LANES), F32),
            jax.ShapeDtypeStruct((surveys, model_count, layer_cells), F32),
        ]
        + [jax.ShapeDtypeStruct((model_count, cells), F32)] * surveys,
        in_specs=[IN_HBM] * 3,
        out_specs=[IN_VMEM] * (5 + surveys),
        scratch_shapes=[
            pltpu.VMEM((slots, block, cells), F32),
            pltpu.VMEM(prior.shape, F32),
            pltpu.VMEM(ids.shape, jnp.int32),
            pltpu.SemaphoreType.DMA((slots,)),
            pltpu.SemaphoreType.DMA((2,)),
        ],
        compiler_params=pltpu.CompilerParams(vmem_limit_bytes=12 * MIB),
        name="prepare",
    )(*[pltpu.with_memory_space_constraint(x, pltpu.HBM) for x in (sens, prior, ids)])
    return *outs[:5], list(outs[5:])


def stepped(models, prior, own, other):
    return models - step_size * ((own + other) + prior_weight * (models - prior))


def forward_kernel(survey, *refs):
    models_ref, prior_ref, own_ref, other_ref, turned_ref = refs[:5]
    models = stepped(models_ref[...], prior_ref[...], own_ref[...], other_ref[...])
    rows = split_rows(models)
    part = fold_rows(dot(rows, turned_ref[0, survey]) + dot(rows, turned_ref[1, survey]))
    refs = refs[5:]
    if survey + 1 < turned_ref.shape[1]:
        next_ref, part_ref = refs
        next_ref[...] = models
        part_ref[...] = part
        return
    earlier_models = refs[:survey]
    earlier_parts = refs[survey : 2 * survey]
    next_ref, edge_ref, part_ref = refs[2 * survey :]
    next_ref[...] = models
    part_ref[survey] = part
    for at in range(survey):
        part_ref[at] = earlier_parts[at][...]
    cells = models.shape[1]
    layer_cells = edge_ref.shape[2]
    downward = lax.axis_index("dp") == 0
    for at, ref in enumerate((*earlier_models, next_ref)):
        edge_ref[at] = jnp.where(
            downward, ref[:, cells - layer_cells :], ref[:, :layer_cells]
        )


def forward(models, prior, owns, others, turned, layer_cells):
    surveys = len(models)
    model_count, _ = models[0].shape
    stations = turned.shape[3]
    moved = []
    parts = []
    for survey in range(surveys):
        out_shape = [jax.ShapeDtypeStruct(models[survey].shape, F32)]
        operands = [models[survey], prior[survey], owns[survey], others[survey], resident(turned)]
        if survey + 1 < surveys:
            out_shape += [jax.ShapeDtypeStruct((model_count, stations), F32)]
        else:
            operands += moved + parts
            out_shape += [
                jax.ShapeDtypeStruct((surveys, model_count, layer_cells), F32),
                jax.ShapeDtypeStruct((surveys, model_count, stations), F32),
            ]
        outs = pl.pallas_call(
            functools.partial(forward_kernel, survey),
            out_shape=out_shape,
            in_specs=[IN_VMEM] * len(operands),
            out_specs=[IN_VMEM] * len(out_shape),
            compiler_params=pltpu.CompilerParams(vmem_limit_bytes=4 * MIB),
            cost_estimate=product_cost(turned),
            name="forward",
        )(*operands)
        moved.append(outs[0])
        parts.append(outs[1])
    return moved, outs[1], outs[2]


def product_cost(split):
    cells = split.shape[2] * split.shape[3]
    return pl.CostEstimate(flops=512 * cells, bytes_accessed=4 * cells, transcendentals=0)


def cross_terms(field, above, keep_x, keep_y, keep_z, depth_only):
    cells = field[0].shape[1]
    first = []
    second = []
    for grads, here, deeper in zip((first, second), field, above):
        grads.append((pltpu.roll(here, cells - 1, 1) - here) * keep_x)
        grads.append((pltpu.roll(here, cells - NX, 1) - here) * keep_y)
        change = deeper - here
        grads.append(change if keep_z is None else change * keep_z)
    cross_x = first[1] * second[2] - first[2] * second[1]
    cross_y = first[2] * second[0] - first[0] * second[2]
    cross_z = first[0] * second[1] - first[1] * second[0]
    scaling = (2.0 * couple_weight) / (
        1.0 + cross_x * cross_x + cross_y * cross_y + cross_z * cross_z
    )
    depth = [
        scaling * (second[0] * cross_y - second[1] * cross_x),
        scaling * (cross_x * first[1] - cross_y * first[0]),
    ]
    if keep_z is not None:
        depth = [value * keep_z for value in depth]
    if depth_only:
        return depth, None
    grad_x = [
        scaling * (second[1] * cross_z - second[2] * cross_y) * keep_x,
        scaling * (cross_y * first[2] - cross_z * first[1]) * keep_x,
    ]
    grad_y = [
        scaling * (second[2] * cross_x - second[0] * cross_z) * keep_y,
        scaling * (cross_z * first[0] - cross_x * first[2]) * keep_y,
    ]
    level = [
        (pltpu.roll(along_x, 1, 1) - along_x) + (pltpu.roll(along_y, NX, 1) - along_y)
        for along_x, along_y in zip(grad_x, grad_y)
    ]
    return depth, level


def couple_kernel(layer_cells, *refs):
    models_refs, edge_ref, out_refs = refs[:2], refs[2], refs[3:]
    model_count, cells = models_refs[0].shape
    layers = cells // layer_cells
    middle = layers // 2
    place = lax.broadcasted_iota(jnp.int32, (model_count, layer_cells), 1)
    keep_x = (place % NX < NX - 1).astype(F32)
    keep_y = (place < layer_cells - NX).astype(F32)
    side = lax.axis_index("dp")
    index = lax.axis_index("cell")

    def layer(at):
        if 0 <= at < layers:
            return [
                ref[:, at * layer_cells : (at + 1) * layer_cells] for ref in models_refs
            ]
        return [edge_ref[survey] for survey in range(2)]

    def write(start, stop):
        sums = {}

        def add(at, values):
            if 0 <= at < layers:
                sums[at] = values if at not in sums else [a + b for a, b in zip(sums[at], values)]

        for at in range(start, stop):
            keep_z = None
            if at < 0:
                keep_z = jnp.where(index > 0, 1.0, 0.0).astype(F32)
            elif at == layers - 1:
                keep_z = jnp.where(index < lax.axis_size("cell") - 1, 1.0, 0.0).astype(F32)
            depth, level = cross_terms(layer(at), layer(at + 1), keep_x, keep_y, keep_z, at < 0)
            if level is not None:
                add(at, [value - below for value, below in zip(level, depth)])
            add(at + 1, depth)
        for at in range(layers):
            for survey in range(2):
                spot = slice(at * layer_cells, (at + 1) * layer_cells)
                if at in sums:
                    out_refs[survey][:, spot] = sums[at][survey]
                else:
                    out_refs[survey][:, spot] = jnp.zeros((model_count, layer_cells), F32)

    @pl.when(side == 0)
    def _():
        write(middle, layers)

    @pl.when(side != 0)
    def _():
        write(-1, middle)


def couple_share(models, edge, layer_cells):
    return pl.pallas_call(
        functools.partial(couple_kernel, layer_cells),
        out_shape=[jax.ShapeDtypeStruct(x.shape, F32) for x in models],
        in_specs=[IN_VMEM] * 3,
        out_specs=[IN_VMEM] * 2,
        compiler_params=pltpu.CompilerParams(vmem_limit_bytes=4 * MIB),
        name="couple",
    )(*models, edge)


def residual_kernel(
    here_ref, there_ref, observed_ref, noise_ref, perturb_ref, ids_ref, count_ref, resid_ref, sums_ref
):
    surveys, model_count, stations = here_ref.shape
    lane = lax.broadcasted_iota(jnp.int32, (model_count, LANES), 1)
    for survey in range(surveys):
        noise = noise_ref[survey : survey + 1]
        targets = observed_ref[survey : survey + 1] + noise * perturb_ref[survey]
        resid = ((here_ref[survey] + there_ref[survey]) - targets) / noise
        resid_ref[survey] = resid
        squares = resid * resid
        ids = jnp.broadcast_to(ids_ref[survey : survey + 1], (model_count, stations))
        sums = count_ref[survey]
        for label in range(NSURV):
            here = jnp.sum(jnp.where(ids == label, squares, 0.0), axis=1, keepdims=True)
            sums = jnp.where(lane == label, here, sums)
        sums_ref[survey] = sums


def residual(here, there, observed, noise, perturb, ids, counts):
    return pl.pallas_call(
        residual_kernel,
        out_shape=[
            jax.ShapeDtypeStruct(here.shape, F32),
            jax.ShapeDtypeStruct(counts.shape, F32),
        ],
        in_specs=[IN_VMEM] * 7,
        out_specs=[IN_VMEM] * 2,
        compiler_params=pltpu.CompilerParams(vmem_limit_bytes=4 * MIB),
        name="residual",
    )(here, there, observed, noise, perturb, ids, counts)


def factor_rows(resid, sums, noise, ids):
    model_count, stations = resid.shape
    counts = pltpu.roll(sums, LANES - NSURV, 1)
    spread = (sums + 1.0) / (counts + 1.0)
    ids = jnp.broadcast_to(ids, (model_count, stations))
    spread_rows = jnp.zeros((model_count, stations), F32)
    for label in range(NSURV):
        spread_rows = jnp.where(ids == label, spread[:, label : label + 1], spread_rows)
    factor = (nu_value + 1.0) * resid / (noise * (nu_value * spread_rows + resid * resid))
    return split_rows(factor)


def spread_gradient(rows, couple_ref, split_ref, survey):
    return couple_ref[...] + fold_rows(
        dot(rows, split_ref[0, survey]) + dot(rows, split_ref[1, survey])
    )


def backward_kernel(
    resid_ref, own_ref, other_ref, noise_ref, ids_ref, couple_ref, split_ref, out_ref, *rows_refs
):
    rows = [
        factor_rows(
            resid_ref[survey],
            own_ref[survey] + other_ref[survey],
            noise_ref[survey : survey + 1],
            ids_ref[survey : survey + 1],
        )
        for survey in range(resid_ref.shape[0])
    ]
    out_ref[...] = spread_gradient(rows[0], couple_ref, split_ref, 0)
    for ref, value in zip(rows_refs, rows[1:]):
        ref[...] = value


def backward_next_kernel(survey, rows_ref, couple_ref, split_ref, out_ref):
    out_ref[...] = spread_gradient(rows_ref[...], couple_ref, split_ref, survey)


def backward(resid, own, other, noise, ids, couple, split):
    surveys, model_count, stations = resid.shape
    params = pltpu.CompilerParams(vmem_limit_bytes=4 * MIB)
    cost = product_cost(split)
    split = resident(split)
    rows_shape = jax.ShapeDtypeStruct((2 * model_count, stations), BF16)
    first, *rows = pl.pallas_call(
        backward_kernel,
        out_shape=[jax.ShapeDtypeStruct(couple[0].shape, F32)] + [rows_shape] * (surveys - 1),
        in_specs=[IN_VMEM] * 7,
        out_specs=[IN_VMEM] * surveys,
        compiler_params=params,
        cost_estimate=cost,
        name="backward",
    )(resid, own, other, noise, ids, couple[0], split)
    grads = [first]
    for survey in range(1, surveys):
        grads.append(
            pl.pallas_call(
                functools.partial(backward_next_kernel, survey),
                out_shape=jax.ShapeDtypeStruct(couple[survey].shape, F32),
                in_specs=[IN_VMEM] * 3,
                out_specs=IN_VMEM,
                compiler_params=params,
                cost_estimate=cost,
                name="backward",
            )(rows[survey - 1], couple[survey], split)
        )
    return grads


def step_kernel(models_ref, prior_ref, own_ref, other_ref, next_ref):
    next_ref[...] = stepped(models_ref[...], prior_ref[...], own_ref[...], other_ref[...])


def finish_kernel(*refs):
    out_ref = refs[-1]
    surveys, _, layers, layer_cells = out_ref.shape
    for survey in range(surveys):
        ready = survey + 1 < surveys
        models = refs[survey][...] if ready else stepped(*[ref[...] for ref in refs[survey:-1]])
        for at in range(layers):
            out_ref[survey, :, at, :] = models[:, at * layer_cells : (at + 1) * layer_cells]


def finish(models, prior, owns, others, shape):
    operands = []
    for survey in range(shape[0]):
        mine = [models[survey], prior[survey], owns[survey], others[survey]]
        if survey + 1 < shape[0]:
            mine = [
                pl.pallas_call(
                    step_kernel,
                    out_shape=jax.ShapeDtypeStruct(models[survey].shape, F32),
                    in_specs=[IN_VMEM] * 4,
                    out_specs=IN_VMEM,
                    compiler_params=pltpu.CompilerParams(vmem_limit_bytes=4 * MIB),
                    name="step",
                )(*mine)
            ]
        operands += mine
    return pl.pallas_call(
        finish_kernel,
        out_shape=jax.ShapeDtypeStruct(shape, F32),
        in_specs=[IN_VMEM] * len(operands),
        out_specs=IN_VMEM,
        compiler_params=pltpu.CompilerParams(vmem_limit_bytes=4 * MIB),
        name="finish",
    )(*operands)


def from_pair(values):
    return lax.ppermute(values, "dp", [(0, 1), (1, 0)])


def exchange_edges(edge):
    devices = lax.axis_size("cell")
    pairs = [(2 * i, 2 * i + 3) for i in range(devices - 1)]
    pairs += [(2 * i + 3, 2 * i) for i in range(devices - 1)]
    return lax.ppermute(edge, ("cell", "dp"), pairs)


def fetch(values, by, devices):
    return lax.ppermute(values, "cell", [(i, i ^ by) for i in range(devices)])


def cell_pair(values):
    devices = lax.axis_size("cell")
    stride = devices
    while stride > 2:
        base = 4 if stride >= 8 else 2
        stride //= base
        total = values
        for count in range(1, base):
            total = total + fetch(values, count * stride, devices)
        values = total
    return values, fetch(values, 1, devices)


def body(sens, observed, noise, ids, data_perturb, prior):
    surveys, _, _, layer_cells = prior.shape
    split, turned, part, counts, edge, flat = prepare(sens, prior, ids)
    models = flat
    for iteration in range(ITERS):
        if iteration:
            models, edge, part = forward(models, flat, owns, others, turned, layer_cells)
        edge = exchange_edges(edge)
        here, there = cell_pair(part)
        couple = couple_share(models, edge, layer_cells)
        resid, own_sums = residual(here, there, observed, noise, data_perturb, ids, counts)
        other_sums = from_pair(own_sums)
        owns = backward(resid, own_sums, other_sums, noise, ids, couple, split)
        others = [from_pair(own) for own in owns]
    return finish(models, flat, owns, others, prior.shape)


def solution(mesh):
    return jax.shard_map(
        body,
        mesh=mesh,
        in_specs=(
            P(None, ("slab", "dp"), "cell"),
            P(None, ("slab", "dp")),
            P(None, ("slab", "dp")),
            P(None, ("slab", "dp")),
            P(None, None, ("slab", "dp")),
            P(None, "slab", "cell", None),
        ),
        out_specs=P(None, "slab", "cell", None),
        check_vma=False,
    )
```

```python
import functools

import jax
import jax.numpy as jnp
from jax import lax
from jax.experimental import pallas as pl
from jax.experimental.pallas import tpu as pltpu
from jax.sharding import PartitionSpec as P

NX = 32
NSURV = 8
ITERS = 4

nu_value = 4.0
step_size = 0.5
couple_weight = 0.02
prior_weight = 0.1

LANES = 128
MIB = 2**20
BF16 = jnp.bfloat16
F32 = jnp.float32
IN_VMEM = pl.BlockSpec(memory_space=pltpu.VMEM)
IN_HBM = pl.BlockSpec(memory_space=pltpu.HBM)


def dot(left, right, along=0):
    return lax.dot_general(
        left, right, (((1,), (along,)), ((), ())), preferred_element_type=F32
    )


def resident(values):
    return pltpu.with_memory_space_constraint(values, pltpu.VMEM)


def split_rows(values):
    high = values.astype(BF16).astype(F32)
    return jnp.concatenate([high, values - high], axis=0).astype(BF16)


def fold_rows(values):
    half = values.shape[0] // 2
    return values[:half] + values[half:]


def prepare_kernel(
    block,
    sens_ref,
    prior_ref,
    ids_ref,
    split_ref,
    turned_ref,
    part_ref,
    count_ref,
    edge_ref,
    *rest,
):
    surveys, stations, _ = sens_ref.shape
    _, model_count, layers, layer_cells = prior_ref.shape
    flat_refs = rest[:surveys]
    buffers, prior_buffer, ids_buffer, semaphores, small_semaphores = rest[surveys:]
    per_survey = stations // block
    total = surveys * per_survey
    slots = buffers.shape[0]

    def copy(step):
        start = pl.multiple_of((step % per_survey) * block, block)
        slot = step % slots
        return pltpu.make_async_copy(
            sens_ref.at[step // per_survey, pl.ds(start, block), :],
            buffers.at[slot],
            semaphores.at[slot],
        )

    prior_copy = pltpu.make_async_copy(prior_ref, prior_buffer, small_semaphores.at[0])
    ids_copy = pltpu.make_async_copy(ids_ref, ids_buffer, small_semaphores.at[1])
    ahead = min(slots - 1, total)
    prior_copy.start()
    ids_copy.start()
    for step in range(min(2, ahead)):
        copy(step).start()
    prior_copy.wait()
    for step in range(min(2, ahead), ahead):
        copy(step).start()
    downward = lax.axis_index("dp") == 0
    for survey in range(surveys):
        layer_rows = [prior_buffer[survey, :, at, :] for at in range(layers)]
        for at in range(layers):
            flat_refs[survey][:, at * layer_cells : (at + 1) * layer_cells] = layer_rows[at]
        edge_ref[survey] = jnp.where(downward, layer_rows[-1], layer_rows[0])
    ids_copy.wait()
    lane = lax.broadcasted_iota(jnp.int32, (model_count, LANES), 1)
    for survey in range(surveys):
        ids = jnp.broadcast_to(ids_buffer[survey : survey + 1], (model_count, stations))
        counts = jnp.zeros((model_count, LANES), F32)
        for label in range(NSURV):
            here = jnp.sum((ids == label).astype(F32), axis=1, keepdims=True)
            counts = jnp.where(lane == NSURV + label, here, counts)
        count_ref[survey] = counts
    for survey in range(surveys):
        rows = split_rows(flat_refs[survey][...])

        def step_fn(at, carry):
            step = survey * per_survey + at
            copy(step).wait()

            @pl.when(step + slots - 1 < total)
            def _():
                copy(step + slots - 1).start()

            place = pl.ds(pl.multiple_of(at * block, block), block)
            values = buffers[step % slots]
            high = values.astype(BF16)
            low = (values - high.astype(F32)).astype(BF16)
            split_ref[0, survey, place, :] = high
            split_ref[1, survey, place, :] = low
            turned = values.T
            high_t = turned.astype(BF16)
            turned_ref[0, survey, :, place] = high_t
            turned_ref[1, survey, :, place] = (turned - high_t.astype(F32)).astype(BF16)
            part_ref[survey, :, place] = fold_rows(dot(rows, high, 1) + dot(rows, low, 1))
            return carry

        lax.fori_loop(0, per_survey, step_fn, 0)


def prepare(sens, prior, ids):
    surveys, stations, cells = sens.shape
    _, model_count, _, layer_cells = prior.shape
    block = min(stations, LANES)
    slots = 5
    outs = pl.pallas_call(
        functools.partial(prepare_kernel, block),
        out_shape=[
            pltpu.VMEM((2, surveys, stations, cells), BF16),
            pltpu.VMEM((2, surveys, cells, stations), BF16),
            jax.ShapeDtypeStruct((surveys, model_count, stations), F32),
            jax.ShapeDtypeStruct((surveys, model_count, LANES), F32),
            jax.ShapeDtypeStruct((surveys, model_count, layer_cells), F32),
        ]
        + [jax.ShapeDtypeStruct((model_count, cells), F32)] * surveys,
        in_specs=[IN_HBM] * 3,
        out_specs=[IN_VMEM] * (5 + surveys),
        scratch_shapes=[
            pltpu.VMEM((slots, block, cells), F32),
            pltpu.VMEM(prior.shape, F32),
            pltpu.VMEM(ids.shape, jnp.int32),
            pltpu.SemaphoreType.DMA((slots,)),
            pltpu.SemaphoreType.DMA((2,)),
        ],
        compiler_params=pltpu.CompilerParams(vmem_limit_bytes=12 * MIB),
        name="prepare",
    )(*[pltpu.with_memory_space_constraint(x, pltpu.HBM) for x in (sens, prior, ids)])
    return *outs[:5], list(outs[5:])


def stepped(models, prior, own, other):
    return models - step_size * ((own + other) + prior_weight * (models - prior))


def forward_kernel(survey, *refs):
    models_ref, prior_ref, own_ref, other_ref, turned_ref = refs[:5]
    models = stepped(models_ref[...], prior_ref[...], own_ref[...], other_ref[...])
    rows = split_rows(models)
    part = fold_rows(dot(rows, turned_ref[0, survey]) + dot(rows, turned_ref[1, survey]))
    refs = refs[5:]
    if survey + 1 < turned_ref.shape[1]:
        next_ref, part_ref = refs
        next_ref[...] = models
        part_ref[...] = part
        return
    earlier_models = refs[:survey]
    earlier_parts = refs[survey : 2 * survey]
    next_ref, edge_ref, part_ref = refs[2 * survey :]
    next_ref[...] = models
    part_ref[survey] = part
    for at in range(survey):
        part_ref[at] = earlier_parts[at][...]
    cells = models.shape[1]
    layer_cells = edge_ref.shape[2]
    downward = lax.axis_index("dp") == 0
    for at, ref in enumerate((*earlier_models, next_ref)):
        edge_ref[at] = jnp.where(
            downward, ref[:, cells - layer_cells :], ref[:, :layer_cells]
        )


def forward(models, prior, owns, others, turned, layer_cells):
    surveys = len(models)
    model_count, _ = models[0].shape
    stations = turned.shape[3]
    moved = []
    parts = []
    for survey in range(surveys):
        out_shape = [jax.ShapeDtypeStruct(models[survey].shape, F32)]
        operands = [models[survey], prior[survey], owns[survey], others[survey], resident(turned)]
        if survey + 1 < surveys:
            out_shape += [jax.ShapeDtypeStruct((model_count, stations), F32)]
        else:
            operands += moved + parts
            out_shape += [
                jax.ShapeDtypeStruct((surveys, model_count, layer_cells), F32),
                jax.ShapeDtypeStruct((surveys, model_count, stations), F32),
            ]
        outs = pl.pallas_call(
            functools.partial(forward_kernel, survey),
            out_shape=out_shape,
            in_specs=[IN_VMEM] * len(operands),
            out_specs=[IN_VMEM] * len(out_shape),
            compiler_params=pltpu.CompilerParams(vmem_limit_bytes=4 * MIB),
            cost_estimate=product_cost(turned),
            name="forward",
        )(*operands)
        moved.append(outs[0])
        parts.append(outs[1])
    return moved, outs[1], outs[2]


def product_cost(split):
    cells = split.shape[2] * split.shape[3]
    return pl.CostEstimate(flops=512 * cells, bytes_accessed=4 * cells, transcendentals=0)


def cross_terms(field, above, keep_x, keep_y, keep_z, depth_only):
    cells = field[0].shape[1]
    first = []
    second = []
    for grads, here, deeper in zip((first, second), field, above):
        grads.append((pltpu.roll(here, cells - 1, 1) - here) * keep_x)
        grads.append((pltpu.roll(here, cells - NX, 1) - here) * keep_y)
        change = deeper - here
        grads.append(change if keep_z is None else change * keep_z)
    cross_x = first[1] * second[2] - first[2] * second[1]
    cross_y = first[2] * second[0] - first[0] * second[2]
    cross_z = first[0] * second[1] - first[1] * second[0]
    scaling = (2.0 * couple_weight) / (
        1.0 + cross_x * cross_x + cross_y * cross_y + cross_z * cross_z
    )
    depth = [
        scaling * (second[0] * cross_y - second[1] * cross_x),
        scaling * (cross_x * first[1] - cross_y * first[0]),
    ]
    if keep_z is not None:
        depth = [value * keep_z for value in depth]
    if depth_only:
        return depth, None
    grad_x = [
        scaling * (second[1] * cross_z - second[2] * cross_y) * keep_x,
        scaling * (cross_y * first[2] - cross_z * first[1]) * keep_x,
    ]
    grad_y = [
        scaling * (second[2] * cross_x - second[0] * cross_z) * keep_y,
        scaling * (cross_z * first[0] - cross_x * first[2]) * keep_y,
    ]
    level = [
        (pltpu.roll(along_x, 1, 1) - along_x) + (pltpu.roll(along_y, NX, 1) - along_y)
        for along_x, along_y in zip(grad_x, grad_y)
    ]
    return depth, level


def couple_kernel(layer_cells, *refs):
    models_refs, edge_ref, out_refs = refs[:2], refs[2], refs[3:]
    model_count, cells = models_refs[0].shape
    layers = cells // layer_cells
    middle = layers // 2
    place = lax.broadcasted_iota(jnp.int32, (model_count, layer_cells), 1)
    keep_x = (place % NX < NX - 1).astype(F32)
    keep_y = (place < layer_cells - NX).astype(F32)
    side = lax.axis_index("dp")
    index = lax.axis_index("cell")

    def layer(at):
        if 0 <= at < layers:
            return [
                ref[:, at * layer_cells : (at + 1) * layer_cells] for ref in models_refs
            ]
        return [edge_ref[survey] for survey in range(2)]

    def write(start, stop):
        sums = {}

        def add(at, values):
            if 0 <= at < layers:
                sums[at] = values if at not in sums else [a + b for a, b in zip(sums[at], values)]

        for at in range(start, stop):
            keep_z = None
            if at < 0:
                keep_z = jnp.where(index > 0, 1.0, 0.0).astype(F32)
            elif at == layers - 1:
                keep_z = jnp.where(index < lax.axis_size("cell") - 1, 1.0, 0.0).astype(F32)
            depth, level = cross_terms(layer(at), layer(at + 1), keep_x, keep_y, keep_z, at < 0)
            if level is not None:
                add(at, [value - below for value, below in zip(level, depth)])
            add(at + 1, depth)
        for at in range(layers):
            for survey in range(2):
                spot = slice(at * layer_cells, (at + 1) * layer_cells)
                if at in sums:
                    out_refs[survey][:, spot] = sums[at][survey]
                else:
                    out_refs[survey][:, spot] = jnp.zeros((model_count, layer_cells), F32)

    @pl.when(side == 0)
    def _():
        write(middle, layers)

    @pl.when(side != 0)
    def _():
        write(-1, middle)


def couple_share(models, edge, layer_cells):
    return pl.pallas_call(
        functools.partial(couple_kernel, layer_cells),
        out_shape=[jax.ShapeDtypeStruct(x.shape, F32) for x in models],
        in_specs=[IN_VMEM] * 3,
        out_specs=[IN_VMEM] * 2,
        compiler_params=pltpu.CompilerParams(vmem_limit_bytes=4 * MIB),
        name="couple",
    )(*models, edge)


def residual_kernel(
    here_ref, there_ref, observed_ref, noise_ref, perturb_ref, ids_ref, count_ref, resid_ref, sums_ref
):
    surveys, model_count, stations = here_ref.shape
    lane = lax.broadcasted_iota(jnp.int32, (model_count, LANES), 1)
    for survey in range(surveys):
        noise = noise_ref[survey : survey + 1]
        targets = observed_ref[survey : survey + 1] + noise * perturb_ref[survey]
        resid = ((here_ref[survey] + there_ref[survey]) - targets) / noise
        resid_ref[survey] = resid
        squares = resid * resid
        ids = jnp.broadcast_to(ids_ref[survey : survey + 1], (model_count, stations))
        sums = count_ref[survey]
        for label in range(NSURV):
            here = jnp.sum(jnp.where(ids == label, squares, 0.0), axis=1, keepdims=True)
            sums = jnp.where(lane == label, here, sums)
        sums_ref[survey] = sums


def residual(here, there, observed, noise, perturb, ids, counts):
    return pl.pallas_call(
        residual_kernel,
        out_shape=[
            jax.ShapeDtypeStruct(here.shape, F32),
            jax.ShapeDtypeStruct(counts.shape, F32),
        ],
        in_specs=[IN_VMEM] * 7,
        out_specs=[IN_VMEM] * 2,
        compiler_params=pltpu.CompilerParams(vmem_limit_bytes=4 * MIB),
        name="residual",
    )(here, there, observed, noise, perturb, ids, counts)


def factor_rows(resid, sums, noise, ids):
    model_count, stations = resid.shape
    counts = pltpu.roll(sums, LANES - NSURV, 1)
    spread = (sums + 1.0) / (counts + 1.0)
    ids = jnp.broadcast_to(ids, (model_count, stations))
    spread_rows = jnp.zeros((model_count, stations), F32)
    for label in range(NSURV):
        spread_rows = jnp.where(ids == label, spread[:, label : label + 1], spread_rows)
    factor = (nu_value + 1.0) * resid / (noise * (nu_value * spread_rows + resid * resid))
    return split_rows(factor)


def spread_gradient(rows, couple_ref, split_ref, survey):
    return couple_ref[...] + fold_rows(
        dot(rows, split_ref[0, survey]) + dot(rows, split_ref[1, survey])
    )


def backward_kernel(
    resid_ref, own_ref, other_ref, noise_ref, ids_ref, couple_ref, split_ref, out_ref, *rows_refs
):
    rows = [
        factor_rows(
            resid_ref[survey],
            own_ref[survey] + other_ref[survey],
            noise_ref[survey : survey + 1],
            ids_ref[survey : survey + 1],
        )
        for survey in range(resid_ref.shape[0])
    ]
    out_ref[...] = spread_gradient(rows[0], couple_ref, split_ref, 0)
    for ref, value in zip(rows_refs, rows[1:]):
        ref[...] = value


def backward_next_kernel(survey, rows_ref, couple_ref, split_ref, out_ref):
    out_ref[...] = spread_gradient(rows_ref[...], couple_ref, split_ref, survey)


def backward(resid, own, other, noise, ids, couple, split):
    surveys, model_count, stations = resid.shape
    params = pltpu.CompilerParams(vmem_limit_bytes=4 * MIB)
    cost = product_cost(split)
    split = resident(split)
    rows_shape = jax.ShapeDtypeStruct((2 * model_count, stations), BF16)
    first, *rows = pl.pallas_call(
        backward_kernel,
        out_shape=[jax.ShapeDtypeStruct(couple[0].shape, F32)] + [rows_shape] * (surveys - 1),
        in_specs=[IN_VMEM] * 7,
        out_specs=[IN_VMEM] * surveys,
        compiler_params=params,
        cost_estimate=cost,
        name="backward",
    )(resid, own, other, noise, ids, couple[0], split)
    grads = [first]
    for survey in range(1, surveys):
        grads.append(
            pl.pallas_call(
                functools.partial(backward_next_kernel, survey),
                out_shape=jax.ShapeDtypeStruct(couple[survey].shape, F32),
                in_specs=[IN_VMEM] * 3,
                out_specs=IN_VMEM,
                compiler_params=params,
                cost_estimate=cost,
                name="backward",
            )(rows[survey - 1], couple[survey], split)
        )
    return grads


def step_kernel(models_ref, prior_ref, own_ref, other_ref, next_ref):
    next_ref[...] = stepped(models_ref[...], prior_ref[...], own_ref[...], other_ref[...])


def finish_kernel(*refs):
    out_ref = refs[-1]
    surveys, _, layers, layer_cells = out_ref.shape
    for survey in range(surveys):
        ready = survey + 1 < surveys
        models = refs[survey][...] if ready else stepped(*[ref[...] for ref in refs[survey:-1]])
        for at in range(layers):
            out_ref[survey, :, at, :] = models[:, at * layer_cells : (at + 1) * layer_cells]


def finish(models, prior, owns, others, shape):
    operands = []
    for survey in range(shape[0]):
        mine = [models[survey], prior[survey], owns[survey], others[survey]]
        if survey + 1 < shape[0]:
            mine = [
                pl.pallas_call(
                    step_kernel,
                    out_shape=jax.ShapeDtypeStruct(models[survey].shape, F32),
                    in_specs=[IN_VMEM] * 4,
                    out_specs=IN_VMEM,
                    compiler_params=pltpu.CompilerParams(vmem_limit_bytes=4 * MIB),
                    name="step",
                )(*mine)
            ]
        operands += mine
    return pl.pallas_call(
        finish_kernel,
        out_shape=jax.ShapeDtypeStruct(shape, F32),
        in_specs=[IN_VMEM] * len(operands),
        out_specs=IN_VMEM,
        compiler_params=pltpu.CompilerParams(vmem_limit_bytes=4 * MIB),
        name="finish",
    )(*operands)


def from_pair(values):
    return lax.ppermute(values, "dp", [(0, 1), (1, 0)])


def exchange_edges(edge):
    devices = lax.axis_size("cell")
    pairs = [(2 * i, 2 * i + 3) for i in range(devices - 1)]
    pairs += [(2 * i + 3, 2 * i) for i in range(devices - 1)]
    return lax.ppermute(edge, ("cell", "dp"), pairs)


def fetch(values, by, devices):
    return lax.ppermute(values, "cell", [(i, i ^ by) for i in range(devices)])


def cell_pair(values):
    devices = lax.axis_size("cell")
    stride = 1
    while devices // stride > 2:
        base = 4 if devices // stride >= 8 else 2
        total = values
        for count in range(1, base):
            total = total + fetch(values, count * stride, devices)
        values = total
        stride *= base
    return values, fetch(values, stride, devices)


def body(sens, observed, noise, ids, data_perturb, prior):
    surveys, _, _, layer_cells = prior.shape
    split, turned, part, counts, edge, flat = prepare(sens, prior, ids)
    models = flat
    for iteration in range(ITERS):
        if iteration:
            models, edge, part = forward(models, flat, owns, others, turned, layer_cells)
        edge = exchange_edges(edge)
        here, there = cell_pair(part)
        couple = couple_share(models, edge, layer_cells)
        resid, own_sums = residual(here, there, observed, noise, data_perturb, ids, counts)
        other_sums = from_pair(own_sums)
        owns = backward(resid, own_sums, other_sums, noise, ids, couple, split)
        others = [from_pair(own) for own in owns]
    return finish(models, flat, owns, others, prior.shape)


def solution(mesh):
    return jax.shard_map(
        body,
        mesh=mesh,
        in_specs=(
            P(None, ("slab", "dp"), "cell"),
            P(None, ("slab", "dp")),
            P(None, ("slab", "dp")),
            P(None, ("slab", "dp")),
            P(None, None, ("slab", "dp")),
            P(None, "slab", "cell", None),
        ),
        out_specs=P(None, "slab", "cell", None),
        check_vma=False,
    )
```

```python
import functools

import jax
import jax.numpy as jnp
from jax import lax
from jax.experimental import pallas as pl
from jax.experimental.pallas import tpu as pltpu
from jax.sharding import PartitionSpec as P

NX = 32
NSURV = 8
ITERS = 4

nu_value = 4.0
step_size = 0.5
couple_weight = 0.02
prior_weight = 0.1

LANES = 128
MIB = 2**20
BF16 = jnp.bfloat16
F32 = jnp.float32
IN_VMEM = pl.BlockSpec(memory_space=pltpu.VMEM)
IN_HBM = pl.BlockSpec(memory_space=pltpu.HBM)


def dot(left, right, along=0):
    return lax.dot_general(
        left, right, (((1,), (along,)), ((), ())), preferred_element_type=F32
    )


def resident(values):
    return pltpu.with_memory_space_constraint(values, pltpu.VMEM)


def split_rows(values):
    high = values.astype(BF16).astype(F32)
    return jnp.concatenate([high, values - high], axis=0).astype(BF16)


def fold_rows(values):
    half = values.shape[0] // 2
    return values[:half] + values[half:]


def prepare_kernel(
    block,
    sens_ref,
    prior_ref,
    ids_ref,
    split_ref,
    turned_ref,
    part_ref,
    count_ref,
    edge_ref,
    *rest,
):
    surveys, stations, _ = sens_ref.shape
    _, model_count, layers, layer_cells = prior_ref.shape
    flat_refs = rest[:surveys]
    buffers, prior_buffer, ids_buffer, semaphores, small_semaphores = rest[surveys:]
    per_survey = stations // block
    total = surveys * per_survey
    slots = buffers.shape[0]

    def copy(step):
        start = pl.multiple_of((step % per_survey) * block, block)
        slot = step % slots
        return pltpu.make_async_copy(
            sens_ref.at[step // per_survey, pl.ds(start, block), :],
            buffers.at[slot],
            semaphores.at[slot],
        )

    prior_copy = pltpu.make_async_copy(prior_ref, prior_buffer, small_semaphores.at[0])
    ids_copy = pltpu.make_async_copy(ids_ref, ids_buffer, small_semaphores.at[1])
    ahead = min(slots - 1, total)
    prior_copy.start()
    ids_copy.start()
    for step in range(min(2, ahead)):
        copy(step).start()
    prior_copy.wait()
    for step in range(min(2, ahead), ahead):
        copy(step).start()
    downward = lax.axis_index("dp") == 0
    for survey in range(surveys):
        layer_rows = [prior_buffer[survey, :, at, :] for at in range(layers)]
        for at in range(layers):
            flat_refs[survey][:, at * layer_cells : (at + 1) * layer_cells] = layer_rows[at]
        edge_ref[survey] = jnp.where(downward, layer_rows[-1], layer_rows[0])
    ids_copy.wait()
    lane = lax.broadcasted_iota(jnp.int32, (model_count, LANES), 1)
    for survey in range(surveys):
        ids = jnp.broadcast_to(ids_buffer[survey : survey + 1], (model_count, stations))
        counts = jnp.zeros((model_count, LANES), F32)
        for label in range(NSURV):
            here = jnp.sum((ids == label).astype(F32), axis=1, keepdims=True)
            counts = jnp.where(lane == NSURV + label, here, counts)
        count_ref[survey] = counts
    for survey in range(surveys):
        rows = split_rows(flat_refs[survey][...])

        def step_fn(at, carry):
            step = survey * per_survey + at
            copy(step).wait()

            @pl.when(step + slots - 1 < total)
            def _():
                copy(step + slots - 1).start()

            place = pl.ds(pl.multiple_of(at * block, block), block)
            values = buffers[step % slots]
            high = values.astype(BF16)
            low = (values - high.astype(F32)).astype(BF16)
            split_ref[0, survey, place, :] = high
            split_ref[1, survey, place, :] = low
            turned = values.T
            high_t = turned.astype(BF16)
            turned_ref[0, survey, :, place] = high_t
            turned_ref[1, survey, :, place] = (turned - high_t.astype(F32)).astype(BF16)
            part_ref[survey, :, place] = fold_rows(dot(rows, high, 1) + dot(rows, low, 1))
            return carry

        lax.fori_loop(0, per_survey, step_fn, 0)


def prepare(sens, prior, ids):
    surveys, stations, cells = sens.shape
    _, model_count, _, layer_cells = prior.shape
    block = min(stations, LANES)
    slots = 5
    outs = pl.pallas_call(
        functools.partial(prepare_kernel, block),
        out_shape=[
            pltpu.VMEM((2, surveys, stations, cells), BF16),
            pltpu.VMEM((2, surveys, cells, stations), BF16),
            jax.ShapeDtypeStruct((surveys, model_count, stations), F32),
            jax.ShapeDtypeStruct((surveys, model_count, LANES), F32),
            jax.ShapeDtypeStruct((surveys, model_count, layer_cells), F32),
        ]
        + [jax.ShapeDtypeStruct((model_count, cells), F32)] * surveys,
        in_specs=[IN_HBM] * 3,
        out_specs=[IN_VMEM] * (5 + surveys),
        scratch_shapes=[
            pltpu.VMEM((slots, block, cells), F32),
            pltpu.VMEM(prior.shape, F32),
            pltpu.VMEM(ids.shape, jnp.int32),
            pltpu.SemaphoreType.DMA((slots,)),
            pltpu.SemaphoreType.DMA((2,)),
        ],
        compiler_params=pltpu.CompilerParams(vmem_limit_bytes=12 * MIB),
        name="prepare",
    )(*[pltpu.with_memory_space_constraint(x, pltpu.HBM) for x in (sens, prior, ids)])
    return *outs[:5], list(outs[5:])


def stepped(models, prior, own, other):
    return models - step_size * ((own + other) + prior_weight * (models - prior))


def forward_kernel(survey, *refs):
    models_ref, prior_ref, own_ref, other_ref, turned_ref = refs[:5]
    models = stepped(models_ref[...], prior_ref[...], own_ref[...], other_ref[...])
    rows = split_rows(models)
    part = fold_rows(dot(rows, turned_ref[0, survey]) + dot(rows, turned_ref[1, survey]))
    refs = refs[5:]
    if survey + 1 < turned_ref.shape[1]:
        next_ref, part_ref = refs
        next_ref[...] = models
        part_ref[...] = part
        return
    earlier_models = refs[:survey]
    earlier_parts = refs[survey : 2 * survey]
    next_ref, edge_ref, part_ref = refs[2 * survey :]
    next_ref[...] = models
    part_ref[survey] = part
    for at in range(survey):
        part_ref[at] = earlier_parts[at][...]
    cells = models.shape[1]
    layer_cells = edge_ref.shape[2]
    downward = lax.axis_index("dp") == 0
    for at, ref in enumerate((*earlier_models, next_ref)):
        edge_ref[at] = jnp.where(
            downward, ref[:, cells - layer_cells :], ref[:, :layer_cells]
        )


def forward(models, prior, owns, others, turned, layer_cells):
    surveys = len(models)
    model_count, _ = models[0].shape
    stations = turned.shape[3]
    moved = []
    parts = []
    for survey in range(surveys):
        out_shape = [jax.ShapeDtypeStruct(models[survey].shape, F32)]
        operands = [models[survey], prior[survey], owns[survey], others[survey], resident(turned)]
        if survey + 1 < surveys:
            out_shape += [jax.ShapeDtypeStruct((model_count, stations), F32)]
        else:
            operands += moved + parts
            out_shape += [
                jax.ShapeDtypeStruct((surveys, model_count, layer_cells), F32),
                jax.ShapeDtypeStruct((surveys, model_count, stations), F32),
            ]
        outs = pl.pallas_call(
            functools.partial(forward_kernel, survey),
            out_shape=out_shape,
            in_specs=[IN_VMEM] * len(operands),
            out_specs=[IN_VMEM] * len(out_shape),
            compiler_params=pltpu.CompilerParams(vmem_limit_bytes=4 * MIB),
            cost_estimate=product_cost(turned),
            name="forward",
        )(*operands)
        moved.append(outs[0])
        parts.append(outs[1])
    return moved, outs[1], outs[2]


def product_cost(split):
    cells = split.shape[2] * split.shape[3]
    return pl.CostEstimate(flops=512 * cells, bytes_accessed=4 * cells, transcendentals=0)


def cross_terms(field, above, keep_x, keep_y, keep_z, depth_only):
    cells = field[0].shape[1]
    first = []
    second = []
    for grads, here, deeper in zip((first, second), field, above):
        grads.append((pltpu.roll(here, cells - 1, 1) - here) * keep_x)
        grads.append((pltpu.roll(here, cells - NX, 1) - here) * keep_y)
        change = deeper - here
        grads.append(change if keep_z is None else change * keep_z)
    cross_x = first[1] * second[2] - first[2] * second[1]
    cross_y = first[2] * second[0] - first[0] * second[2]
    cross_z = first[0] * second[1] - first[1] * second[0]
    scaling = (2.0 * couple_weight) / (
        1.0 + cross_x * cross_x + cross_y * cross_y + cross_z * cross_z
    )
    depth = [
        scaling * (second[0] * cross_y - second[1] * cross_x),
        scaling * (cross_x * first[1] - cross_y * first[0]),
    ]
    if keep_z is not None:
        depth = [value * keep_z for value in depth]
    if depth_only:
        return depth, None
    grad_x = [
        scaling * (second[1] * cross_z - second[2] * cross_y) * keep_x,
        scaling * (cross_y * first[2] - cross_z * first[1]) * keep_x,
    ]
    grad_y = [
        scaling * (second[2] * cross_x - second[0] * cross_z) * keep_y,
        scaling * (cross_z * first[0] - cross_x * first[2]) * keep_y,
    ]
    level = [
        (pltpu.roll(along_x, 1, 1) - along_x) + (pltpu.roll(along_y, NX, 1) - along_y)
        for along_x, along_y in zip(grad_x, grad_y)
    ]
    return depth, level


def couple_kernel(layer_cells, *refs):
    models_refs, edge_ref, out_refs = refs[:2], refs[2], refs[3:]
    model_count, cells = models_refs[0].shape
    layers = cells // layer_cells
    middle = layers // 2
    place = lax.broadcasted_iota(jnp.int32, (model_count, layer_cells), 1)
    keep_x = (place % NX < NX - 1).astype(F32)
    keep_y = (place < layer_cells - NX).astype(F32)
    side = lax.axis_index("dp")
    index = lax.axis_index("cell")

    def layer(at):
        if 0 <= at < layers:
            return [
                ref[:, at * layer_cells : (at + 1) * layer_cells] for ref in models_refs
            ]
        return [edge_ref[survey] for survey in range(2)]

    def write(start, stop):
        sums = {}

        def add(at, values):
            if 0 <= at < layers:
                sums[at] = values if at not in sums else [a + b for a, b in zip(sums[at], values)]

        for at in range(start, stop):
            keep_z = None
            if at < 0:
                keep_z = jnp.where(index > 0, 1.0, 0.0).astype(F32)
            elif at == layers - 1:
                keep_z = jnp.where(index < lax.axis_size("cell") - 1, 1.0, 0.0).astype(F32)
            depth, level = cross_terms(layer(at), layer(at + 1), keep_x, keep_y, keep_z, at < 0)
            if level is not None:
                add(at, [value - below for value, below in zip(level, depth)])
            add(at + 1, depth)
        for at in range(layers):
            for survey in range(2):
                spot = slice(at * layer_cells, (at + 1) * layer_cells)
                if at in sums:
                    out_refs[survey][:, spot] = sums[at][survey]
                else:
                    out_refs[survey][:, spot] = jnp.zeros((model_count, layer_cells), F32)

    @pl.when(side == 0)
    def _():
        write(middle, layers)

    @pl.when(side != 0)
    def _():
        write(-1, middle)


def couple_share(models, edge, layer_cells):
    return pl.pallas_call(
        functools.partial(couple_kernel, layer_cells),
        out_shape=[jax.ShapeDtypeStruct(x.shape, F32) for x in models],
        in_specs=[IN_VMEM] * 3,
        out_specs=[IN_VMEM] * 2,
        compiler_params=pltpu.CompilerParams(vmem_limit_bytes=4 * MIB),
        name="couple",
    )(*models, edge)


def residual_kernel(
    here_ref, there_ref, observed_ref, noise_ref, perturb_ref, ids_ref, count_ref, resid_ref, sums_ref
):
    surveys, model_count, stations = here_ref.shape
    lane = lax.broadcasted_iota(jnp.int32, (model_count, LANES), 1)
    for survey in range(surveys):
        noise = noise_ref[survey : survey + 1]
        targets = observed_ref[survey : survey + 1] + noise * perturb_ref[survey]
        resid = ((here_ref[survey] + there_ref[survey]) - targets) / noise
        resid_ref[survey] = resid
        squares = resid * resid
        ids = jnp.broadcast_to(ids_ref[survey : survey + 1], (model_count, stations))
        sums = count_ref[survey]
        for label in range(NSURV):
            here = jnp.sum(jnp.where(ids == label, squares, 0.0), axis=1, keepdims=True)
            sums = jnp.where(lane == label, here, sums)
        sums_ref[survey] = sums


def residual(here, there, observed, noise, perturb, ids, counts):
    return pl.pallas_call(
        residual_kernel,
        out_shape=[
            jax.ShapeDtypeStruct(here.shape, F32),
            jax.ShapeDtypeStruct(counts.shape, F32),
        ],
        in_specs=[IN_VMEM] * 7,
        out_specs=[IN_VMEM] * 2,
        compiler_params=pltpu.CompilerParams(vmem_limit_bytes=4 * MIB),
        name="residual",
    )(here, there, observed, noise, perturb, ids, counts)


def factor_rows(resid, sums, noise, ids):
    model_count, stations = resid.shape
    counts = pltpu.roll(sums, LANES - NSURV, 1)
    spread = (sums + 1.0) / (counts + 1.0)
    ids = jnp.broadcast_to(ids, (model_count, stations))
    spread_rows = jnp.zeros((model_count, stations), F32)
    for label in range(NSURV):
        spread_rows = jnp.where(ids == label, spread[:, label : label + 1], spread_rows)
    factor = (nu_value + 1.0) * resid / (noise * (nu_value * spread_rows + resid * resid))
    return split_rows(factor)


def spread_gradient(rows, couple_ref, split_ref, survey):
    return couple_ref[...] + fold_rows(
        dot(rows, split_ref[0, survey]) + dot(rows, split_ref[1, survey])
    )


def backward_kernel(
    resid_ref, own_ref, other_ref, noise_ref, ids_ref, couple_ref, split_ref, out_ref, *rows_refs
):
    rows = [
        factor_rows(
            resid_ref[survey],
            own_ref[survey] + other_ref[survey],
            noise_ref[survey : survey + 1],
            ids_ref[survey : survey + 1],
        )
        for survey in range(resid_ref.shape[0])
    ]
    out_ref[...] = spread_gradient(rows[0], couple_ref, split_ref, 0)
    for ref, value in zip(rows_refs, rows[1:]):
        ref[...] = value


def backward_next_kernel(survey, start, rows_ref, couple_ref, split_ref, out_ref):
    spot = slice(start, start + out_ref.shape[1])
    rows = rows_ref[...]
    out_ref[...] = couple_ref[:, spot] + fold_rows(
        dot(rows, split_ref[0, survey, :, spot]) + dot(rows, split_ref[1, survey, :, spot])
    )


def backward(resid, own, other, noise, ids, couple, split, pieces):
    surveys, model_count, stations = resid.shape
    params = pltpu.CompilerParams(vmem_limit_bytes=4 * MIB)
    cost = product_cost(split)
    split = resident(split)
    rows_shape = jax.ShapeDtypeStruct((2 * model_count, stations), BF16)
    first, *rows = pl.pallas_call(
        backward_kernel,
        out_shape=[jax.ShapeDtypeStruct(couple[0].shape, F32)] + [rows_shape] * (surveys - 1),
        in_specs=[IN_VMEM] * 7,
        out_specs=[IN_VMEM] * surveys,
        compiler_params=params,
        cost_estimate=cost,
        name="backward",
    )(resid, own, other, noise, ids, couple[0], split)
    grads = [first]
    for survey, at in [(s, p) for s in range(1, surveys) for p in range(pieces)]:
        width = couple[survey].shape[1] // pieces
        grads.append(
            pl.pallas_call(
                functools.partial(backward_next_kernel, survey, at * width),
                out_shape=jax.ShapeDtypeStruct((model_count, width), F32),
                in_specs=[IN_VMEM] * 3,
                out_specs=IN_VMEM,
                compiler_params=params,
                cost_estimate=cost,
                name="backward",
            )(rows[survey - 1], couple[survey], split)
        )
    return grads


def step_kernel(models_ref, prior_ref, own_ref, other_ref, next_ref):
    next_ref[...] = stepped(models_ref[...], prior_ref[...], own_ref[...], other_ref[...])


def finish_kernel(*refs):
    out_ref = refs[-1]
    surveys, _, layers, layer_cells = out_ref.shape
    for survey in range(surveys):
        ready = survey + 1 < surveys
        if ready:
            models = refs[survey][...]
        else:
            tail = [ref[...] for ref in refs[survey + 2 : -1]]
            half = len(tail) // 2
            sides = [jnp.concatenate(x, axis=1) for x in (tail[:half], tail[half:])]
            models = stepped(refs[survey][...], refs[survey + 1][...], *sides)
        for at in range(layers):
            out_ref[survey, :, at, :] = models[:, at * layer_cells : (at + 1) * layer_cells]


def finish(models, prior, owns, others, shape):
    operands = []
    for survey in range(shape[0]):
        mine = [models[survey], prior[survey]]
        if survey + 1 == shape[0]:
            mine += [*owns[survey:], *others[survey:]]
        else:
            mine += [owns[survey], others[survey]]
            mine = [
                pl.pallas_call(
                    step_kernel,
                    out_shape=jax.ShapeDtypeStruct(models[survey].shape, F32),
                    in_specs=[IN_VMEM] * 4,
                    out_specs=IN_VMEM,
                    compiler_params=pltpu.CompilerParams(vmem_limit_bytes=4 * MIB),
                    name="step",
                )(*mine)
            ]
        operands += mine
    return pl.pallas_call(
        finish_kernel,
        out_shape=jax.ShapeDtypeStruct(shape, F32),
        in_specs=[IN_VMEM] * len(operands),
        out_specs=IN_VMEM,
        compiler_params=pltpu.CompilerParams(vmem_limit_bytes=4 * MIB),
        name="finish",
    )(*operands)


def from_pair(values):
    return lax.ppermute(values, "dp", [(0, 1), (1, 0)])


def exchange_edges(edge):
    devices = lax.axis_size("cell")
    pairs = [(2 * i, 2 * i + 3) for i in range(devices - 1)]
    pairs += [(2 * i + 3, 2 * i) for i in range(devices - 1)]
    return lax.ppermute(edge, ("cell", "dp"), pairs)


def fetch(values, by, devices):
    return lax.ppermute(values, "cell", [(i, i ^ by) for i in range(devices)])


def cell_pair(values):
    devices = lax.axis_size("cell")
    stride = 1
    while devices // stride > 2:
        base = 4 if devices // stride >= 8 else 2
        total = values
        for count in range(1, base):
            total = total + fetch(values, count * stride, devices)
        values = total
        stride *= base
    return values, fetch(values, stride, devices)


def body(sens, observed, noise, ids, data_perturb, prior):
    surveys, _, _, layer_cells = prior.shape
    split, turned, part, counts, edge, flat = prepare(sens, prior, ids)
    models = flat
    for iteration in range(ITERS):
        if iteration:
            models, edge, part = forward(models, flat, owns, others, turned, layer_cells)
        edge = exchange_edges(edge)
        here, there = cell_pair(part)
        couple = couple_share(models, edge, layer_cells)
        resid, own_sums = residual(here, there, observed, noise, data_perturb, ids, counts)
        other_sums = from_pair(own_sums)
        owns = backward(resid, own_sums, other_sums, noise, ids, couple, split, 1 if iteration + 1 < ITERS else 2)
        others = [from_pair(own) for own in owns]
    return finish(models, flat, owns, others, prior.shape)


def solution(mesh):
    return jax.shard_map(
        body,
        mesh=mesh,
        in_specs=(
            P(None, ("slab", "dp"), "cell"),
            P(None, ("slab", "dp")),
            P(None, ("slab", "dp")),
            P(None, ("slab", "dp")),
            P(None, None, ("slab", "dp")),
            P(None, "slab", "cell", None),
        ),
        out_specs=P(None, "slab", "cell", None),
        check_vma=False,
    )
```
